128 devices in a mesh: seq: 16 (over x, z), fsdp: 8 (over y, core).
Axes of the slice: x: 4, y: 4, z: 4, core: 2. Of those that a mesh axis runs over, the one named last changes fastest.
Arguments:
- queries: bfloat16 [8, 6144, 2048], P('fsdp', 'seq'), may hold values from -16 to 16
- key_states: bfloat16 [8, 6144, 2048], P('fsdp', 'seq'), may hold values from -16 to 16
- value_states: bfloat16 [8, 6144, 2048], P('fsdp', 'seq'), may hold values from -6 to 6
- residual: bfloat16 [8, 6144, 3072], P('fsdp', 'seq'), may hold values from -6 to 6
- upstream: bfloat16 [8, 6144, 3072], P('fsdp', 'seq'), may hold values from -6 to 6
- mod_gate: float32 [8, 3072], P('fsdp'), may hold values from 0.5 to 1.5
- out_bias: float32 [3072], replicated, may hold values from -3 to 3
- w_out: bfloat16 [2048, 3072], P('fsdp'), may hold values from -0.125 to 0.125
- neighbours: int32 [48, 9], replicated, may hold values from 0 to 47, as said below
- counts: int32 [48], replicated, may hold values from 3 to 9, as said below
- text_tiles: int32 [4], replicated, may hold values from 0 to 47, as said below
Outputs:
- block_out: bfloat16 [8, 6144, 3072], P('fsdp', 'seq')
- grad_queries: bfloat16 [8, 6144, 2048], P('fsdp', 'seq')
- grad_keys: bfloat16 [8, 6144, 2048], P('fsdp', 'seq')
- grad_values: bfloat16 [8, 6144, 2048], P('fsdp', 'seq')
The draws below stay inside these ranges and needn't reach their ends.
Inputs may be any that keep to these rules, and one draw needn't show every extreme that they name: `neighbours`: each query tile that holds image tokens lists first, in its counts slots, the distinct image tiles within one row and one column of its own place in the image, itself included; the image tiles are the tiles not in text_tiles, in increasing order, laid out row by row with 8 to a row. A text tile lists 9 distinct image tiles. Slots at or after counts hold arbitrary image tiles. `counts`: every text tile has 9. `text_tiles`: Distinct, in increasing order; the last tile of a sequence is always one of them.
All inputs are finite; a program needn't handle non-finite values.
Results may differ from the reference program's by a relative error of at most 0.023.
Values may be sent and summed in bfloat16 or wider, within the bound.
A program may use at most 128 MiB of HBM per device.

```python
import math
import jax
import jax.numpy as jnp
from jax import lax

D = 3072
HD = 128
HEADS = 16
TILE = 128
GW = 8
NBR_MAX = 9
TXT_TILES = 4
SEQ = 6144
TILES = 48
BATCH = 8
HDT = 2048


def neighbour_table(key):
    image_count = TILES - TXT_TILES
    order = jax.random.permutation(jax.random.fold_in(key, 100), TILES - 1)
    text_ids = jnp.sort(jnp.concatenate([order[:TXT_TILES - 1], jnp.array([TILES - 1], dtype=order.dtype)])).astype(jnp.int32)
    spots = jnp.arange(TILES, dtype=jnp.int32)
    is_text = jnp.any(spots[:, None] == text_ids[None, :], axis=1)
    image_ids = jnp.sort(jnp.where(is_text, TILES + spots, spots))[:image_count].astype(jnp.int32)
    rank = jnp.cumsum(jnp.where(is_text, 0, 1)).astype(jnp.int32) - 1
    grid_row = rank // GW
    grid_col = rank % GW
    shift_row = jnp.array([-1, -1, -1, 0, 0, 0, 1, 1, 1], dtype=jnp.int32)
    shift_col = jnp.array([-1, 0, 1, -1, 0, 1, -1, 0, 1], dtype=jnp.int32)
    near_row = grid_row[:, None] + shift_row[None, :]
    near_col = grid_col[:, None] + shift_col[None, :]
    near_rank = near_row * GW + near_col
    usable = (near_row >= 0) & (near_col >= 0) & (near_col < GW) & (near_rank < image_count)
    slot_ids = jnp.arange(NBR_MAX, dtype=jnp.int32)
    ranking = jnp.argsort(jnp.where(usable, 0, NBR_MAX) + slot_ids[None, :], axis=1)
    near_rank = jnp.take_along_axis(near_rank, ranking, axis=1)
    usable = jnp.take_along_axis(usable, ranking, axis=1)
    filler = jax.random.randint(jax.random.fold_in(key, 101), (TILES, NBR_MAX), 0, image_count)
    image_pick = jnp.where(usable, near_rank, filler)
    text_key = jax.random.fold_in(key, 102)
    text_pick = jax.vmap(lambda spot: jax.random.permutation(jax.random.fold_in(text_key, spot), image_count)[:NBR_MAX])(spots)
    chosen = jnp.where(is_text[:, None], text_pick, image_pick).astype(jnp.int32)
    listing = image_ids[chosen].astype(jnp.int32)
    tallies = jnp.where(is_text, NBR_MAX, jnp.sum(usable.astype(jnp.int32), axis=1)).astype(jnp.int32)
    return (listing, tallies, text_ids)


def draw_neighbours(key, part):
    listing, tallies, text_ids = neighbour_table(key)
    return listing


def draw_counts(key, part):
    listing, tallies, text_ids = neighbour_table(key)
    return tallies


def draw_text_tiles(key, part):
    listing, tallies, text_ids = neighbour_table(key)
    return text_ids


def draw_queries(key, part):
    key = jax.random.fold_in(key, 21)
    return jax.random.truncated_normal(key, -6.0, 6.0, (BATCH, SEQ, HEADS * HD)).astype(jnp.bfloat16)


def draw_key_states(key, part):
    key = jax.random.fold_in(key, 22)
    return jax.random.truncated_normal(key, -6.0, 6.0, (BATCH, SEQ, HEADS * HD)).astype(jnp.bfloat16)


def levels(key, shape, shards, smallest, high):
    loudness = 1.0
    for axis_at, parts in shards:
        draws = jax.random.uniform(jax.random.fold_in(jax.random.fold_in(key, 6), axis_at), (parts,), jnp.float32, smallest / len(shards), high / len(shards))
        loudness = loudness * jnp.repeat(jnp.exp(draws), shape[axis_at] // parts).reshape((-1,) + (1,) * (len(shape) - 1 - axis_at))
    return loudness


def bell_draw(key, dims, scale, most, split=(), held_as=jnp.bfloat16):
    drawn = jax.random.normal(key, dims, jnp.float32) * scale
    if len(split) > 0:
        drawn = levels(key, dims, split, -0.22, 0.18) * drawn
    return jnp.clip(drawn, min=-most, max=most).astype(held_as)


def setup_inputs(seed: int = 0) -> dict:
    streams_of = jax.random.split(jax.random.key(seed), 12)
    queries = draw_queries(jax.random.fold_in(streams_of[11], 71), 0)
    key_states = draw_key_states(jax.random.fold_in(streams_of[11], 71), 0)
    value_states = bell_draw(streams_of[2], (BATCH, SEQ, HDT), 1.0, 6.0, ((0, 8), (1, 16)))
    residual = bell_draw(streams_of[3], (BATCH, SEQ, D), 1.0, 6.0, ((0, 8), (1, 16)))
    upstream = bell_draw(streams_of[4], (BATCH, SEQ, D), 1.0, 6.0, ((0, 8), (1, 16)))
    mod_gate = jnp.clip(0.5 + 1.0 * jax.random.uniform(streams_of[5], (BATCH, D), jnp.float32) ** levels(streams_of[5], (BATCH, D), ((0, 8),), -0.2, 0.2), 0.5, 1.5)
    out_bias = bell_draw(streams_of[6], (D,), 0.5, 3.0, (), jnp.float32)
    w_out = bell_draw(streams_of[7], (HDT, D), HDT ** -0.5, 0.125, ((0, 8),))
    neighbours = draw_neighbours(jax.random.fold_in(streams_of[11], 71), 0)
    counts = draw_counts(jax.random.fold_in(streams_of[11], 71), 0)
    text_tiles = draw_text_tiles(jax.random.fold_in(streams_of[11], 71), 0)
    return {"queries": queries, "key_states": key_states, "value_states": value_states, "residual": residual, "upstream": upstream, "mod_gate": mod_gate, "out_bias": out_bias, "w_out": w_out, "neighbours": neighbours, "counts": counts, "text_tiles": text_tiles}


def key_layout(neighbours, counts, text_tiles):
    tile_count = neighbours.shape[0]
    slot_count = neighbours.shape[1]
    text_count = text_tiles.shape[0]
    listing = jnp.concatenate([neighbours.astype(jnp.int32), jnp.broadcast_to(text_tiles.astype(jnp.int32)[None, :], (tile_count, text_count))], axis=1)
    nearby = jnp.arange(slot_count, dtype=jnp.int32)[None, :] < counts.astype(jnp.int32)[:, None]
    live_slots = jnp.concatenate([nearby, jnp.ones((tile_count, text_count), dtype=jnp.bool_)], axis=1)
    return (listing, live_slots)

def sequence_pass(query_tiles, key_tiles, value_tiles, upstream_tiles, listing, live_slots, tile_group):
    tile_count, tile_len, head_count, head_dim = query_tiles.shape
    factor = 1.0 / math.sqrt(head_dim)

    def one_group(sums_in, group_start):
        key_sum, value_sum = sums_in
        query_part = lax.dynamic_slice_in_dim(query_tiles, group_start, tile_group, 0).astype(jnp.float32)
        upstream_part = lax.dynamic_slice_in_dim(upstream_tiles, group_start, tile_group, 0).astype(jnp.float32)
        picked = lax.dynamic_slice_in_dim(listing, group_start, tile_group, 0)
        alive_slots = lax.dynamic_slice_in_dim(live_slots, group_start, tile_group, 0)
        key_near = key_tiles[picked].astype(jnp.float32)
        value_near = value_tiles[picked].astype(jnp.float32)
        scores = jnp.einsum('qthe,qkshe->qhtks', query_part, key_near) * factor
        scores = jnp.where(alive_slots[:, None, None, :, None], scores, -jnp.inf)
        row_max = lax.optimization_barrier(jnp.max(scores, axis=(3, 4), keepdims=True))
        exponent = jnp.exp(scores - row_max)
        attn_prob = exponent / lax.optimization_barrier(jnp.sum(exponent, axis=(3, 4), keepdims=True))
        prob_half = attn_prob.astype(jnp.bfloat16)
        attended = jnp.einsum('qhtks,qkshe->qthe', prob_half.astype(jnp.float32), value_near).astype(jnp.bfloat16)
        row_delta = lax.optimization_barrier(jnp.sum(upstream_part * attended.astype(jnp.float32), axis=3))
        row_delta = jnp.transpose(row_delta, (0, 2, 1))[:, :, :, None, None]
        prob_grad = jnp.einsum('qthe,qkshe->qhtks', upstream_part, value_near)
        score_grad = (attn_prob * (prob_grad - row_delta) * factor).astype(jnp.bfloat16).astype(jnp.float32)
        grad_query = jnp.einsum('qhtks,qkshe->qthe', score_grad, key_near).astype(jnp.bfloat16)
        key_terms = jnp.einsum('qhtks,qthe->qkshe', score_grad, query_part)
        value_terms = jnp.einsum('qhtks,qthe->qkshe', prob_half.astype(jnp.float32), upstream_part)
        flat_ids = picked.reshape(-1)
        key_sum = key_sum.at[flat_ids].add(key_terms.reshape(-1, tile_len, head_count, head_dim))
        value_sum = value_sum.at[flat_ids].add(value_terms.reshape(-1, tile_len, head_count, head_dim))
        return ((key_sum, value_sum), (attended, grad_query))
    zeros_sum = jnp.zeros((tile_count, tile_len, head_count, head_dim), jnp.float32)
    group_starts = jnp.arange(0, tile_count, tile_group, dtype=jnp.int32)
    (key_sum, value_sum), (attended, grad_query) = lax.scan(one_group, (zeros_sum, zeros_sum), group_starts)
    row_total = tile_count * tile_len
    feature_total = head_count * head_dim
    return (attended.reshape(row_total, feature_total), grad_query.reshape(row_total, feature_total), key_sum.astype(jnp.bfloat16).reshape(row_total, feature_total), value_sum.astype(jnp.bfloat16).reshape(row_total, feature_total))

def reference(queries, key_states, value_states, residual, upstream, mod_gate, out_bias, w_out, neighbours, counts, text_tiles):
    seq_count, seq_len, feature_total = queries.shape
    width = w_out.shape[1]
    tile_count = seq_len // TILE
    tile_group = math.gcd(tile_count, max(1, 512 // TILE))
    listing, live_slots = key_layout(neighbours, counts, text_tiles)
    scaled = (upstream.astype(jnp.float32) * mod_gate[:, None, :]).astype(jnp.bfloat16)
    d_attn = jnp.dot(scaled.reshape(seq_count * seq_len, width), jnp.transpose(w_out), preferred_element_type=jnp.float32)
    d_attn = d_attn.astype(jnp.bfloat16).reshape(seq_count, seq_len, feature_total)

    def as_tiles(array_in):
        return array_in.reshape(tile_count, TILE, HEADS, HD)

    def per_sequence(inputs):
        query_seq, key_seq, value_seq, upstream_seq = inputs
        return sequence_pass(as_tiles(query_seq), as_tiles(key_seq), as_tiles(value_seq), as_tiles(upstream_seq), listing, live_slots, tile_group)
    attended, grad_query, grad_key, grad_value = lax.map(per_sequence, (queries, key_states, value_states, d_attn))
    projected = jnp.dot(attended.reshape(seq_count * seq_len, feature_total), w_out, preferred_element_type=jnp.float32)
    projected = projected.reshape(seq_count, seq_len, width)
    block_out = (residual.astype(jnp.float32) + mod_gate[:, None, :] * (projected + out_bias[None, None, :])).astype(jnp.bfloat16)
    return (block_out, grad_query, grad_key, grad_value)
```

```python
import math
import jax, jax.numpy as jnp
from jax import lax
from jax.experimental import pallas as pl
from jax.experimental.pallas import tpu as pltpu
from jax.sharding import PartitionSpec as P

HD=128; TILE=128; TILES=48; NBR=9; TXT=4; SLOTS=13
FACTOR = 1.0/math.sqrt(HD)
EXP2 = FACTOR*math.log2(math.e)
F32=jnp.float32; BF=jnp.bfloat16

def tables(neighbours, counts, text_tiles):
    ids = jnp.arange(TILES, dtype=jnp.int32)
    slot = jnp.arange(NBR, dtype=jnp.int32)
    live = slot[None, :] < counts[:, None]
    near = jnp.where(live, neighbours, neighbours[:, :1])
    keys = jnp.concatenate([near, jnp.broadcast_to(text_tiles[None, :], (TILES, TXT))], axis=1)
    bias = jnp.where(live, 0.0, -jnp.inf).astype(F32)
    hit = (neighbours[:, :, None] == ids[None, None, :]) & live[:, :, None]
    block = jnp.sum(jnp.where(hit, (slot[None, :, None] + 1) + SLOTS * ids[:, None, None], 0), axis=1)
    is_text = jnp.any(ids[:, None] == text_tiles[None, :], axis=1)
    who = jnp.concatenate([near, jnp.broadcast_to(text_tiles[None, :], (TILES, TXT))], axis=1)
    ok = jnp.concatenate([live, jnp.ones((TILES, TXT), jnp.bool_)], axis=1) & ~is_text[:, None]
    pick = jnp.sum(jnp.where(who[:, :, None] == ids[None, None, :], block.T[:, None, :], 0), axis=2)
    pidx = jnp.where(ok & (pick > 0), pick - 1, TILES * SLOTS)
    tsel = jnp.min(jnp.where(ids[:, None] == text_tiles[None, :], jnp.arange(TXT, dtype=jnp.int32)[None, :], TXT), axis=1)
    return keys, bias, pidx, tsel

def tile(ref, i):
    return ref[pl.ds(pl.multiple_of(i * TILE, TILE), TILE), :]

NT = (((1,), (1,)), ((), ()))
NN = (((1,), (0,)), ((), ()))

def dot(a, b, dims=NN):
    return lax.dot_general(a, b, dims, preferred_element_type=F32)

def fwd_tile(i, q_ref, k_ref, vt_ref, keys_ref, bias_ref, p_ref, s_ref, inv_ref, attn_ref):
    q = tile(q_ref, i)
    top = None
    kc = jnp.concatenate([tile(k_ref, keys_ref[i, s]) for s in range(SLOTS)], axis=0)
    sall = dot(kc, q, NT).reshape(SLOTS, TILE, TILE)
    for s in range(SLOTS):
        sc = sall[s]
        s_ref[s] = sc
        top = sc if top is None else jnp.maximum(top, sc)
    m = jnp.max(top, axis=0, keepdims=True) * EXP2
    total = None
    parts = []
    for s in range(SLOTS):
        shift = m if s < 3 or s >= NBR else m - bias_ref[i, s]
        e = jnp.exp2(s_ref[s] * EXP2 - shift)
        total = e if total is None else total + e
        e16 = e.astype(BF)
        p_ref[i * SLOTS + s] = e16
        parts.append(e16)
    inv = 1.0 / jnp.sum(total, axis=0, keepdims=True)
    inv_ref[i] = inv
    pt = jnp.concatenate(parts, axis=0)
    vt = jnp.concatenate([vt_ref[keys_ref[i, s]] for s in range(SLOTS)], axis=1)
    attn_t = dot(vt, pt) * inv
    attn_ref[pl.ds(pl.multiple_of(i * TILE, TILE), TILE), :] = attn_t.astype(BF).T

def key_tile(j, who_ref, pidx_ref, tsel_ref, p_ref, x_ref, text_ref, out_ref):
    lhs = jnp.concatenate([p_ref[pidx_ref[j, r]] for r in range(SLOTS)], axis=1)
    rhs = jnp.concatenate([tile(x_ref, who_ref[j, r]) for r in range(SLOTS)], axis=0)
    acc = dot(lhs, rhs) + text_ref[tsel_ref[j]]
    out_ref[pl.ds(pl.multiple_of(j * TILE, TILE), TILE), :] = acc.astype(BF)

def text_keys(p_ref, x_ref, text_ref):
    G = 12
    text_ref[...] = jnp.zeros_like(text_ref)
    def body(g, _):
        rhs = x_ref[pl.ds(pl.multiple_of(g * G * TILE, TILE), G * TILE), :]
        for u in range(TXT):
            lhs = jnp.concatenate([p_ref[(g * G + n) * SLOTS + NBR + u] for n in range(G)], axis=1)
            text_ref[u] += dot(lhs, rhs)
        return 0
    lax.fori_loop(0, TILES // G, body, 0)

def bwd_tile(i, v_ref, kt_ref, do_ref, attn_ref, keys_ref, p_ref, inv_ref, dq_ref):
    do = tile(do_ref, i)
    prod = do.astype(F32) * tile(attn_ref, i).astype(F32)
    delta = jnp.sum(prod.T, axis=0, keepdims=True)
    c = inv_ref[i] * FACTOR
    dc = delta * c
    vc = jnp.concatenate([tile(v_ref, keys_ref[i, s]) for s in range(SLOTS)], axis=0)
    dpall = dot(vc, do, NT).reshape(SLOTS, TILE, TILE)
    parts = [(p_ref[i * SLOTS + s].astype(F32) * (dpall[s] * c - dc)).astype(BF) for s in range(SLOTS)]
    for s in range(SLOTS): p_ref[i * SLOTS + s] = parts[s]
    ds = jnp.concatenate(parts, axis=0)
    kt = jnp.concatenate([kt_ref[keys_ref[i, s]] for s in range(SLOTS)], axis=1)
    dq_t = dot(kt, ds)
    dq_ref[pl.ds(pl.multiple_of(i * TILE, TILE), TILE), :] = dq_t.astype(BF).T

def scale_rows(i, do_ref, inv_ref, dos_ref):
    col = jnp.broadcast_to(inv_ref[i], (TILE, TILE)).T
    sl = pl.ds(pl.multiple_of(i * TILE, TILE), TILE)
    dos_ref[sl, :] = (do_ref[sl, :].astype(F32) * col).astype(BF)

def attn_kernel(keys_ref, bias_ref, pidx_ref, tsel_ref, q_ref, k_ref, v_ref, do_ref, attn_ref, dq_ref, dk_ref, dv_ref,
                p_ref, s_ref, kt_ref, vt_ref, inv_ref, text_ref, dos_ref):
    p_ref[TILES * SLOTS] = jnp.zeros((TILE, TILE), BF)
    def loop(n, f, unroll=1):
        lax.fori_loop(0, n, lambda i, _: (f(i), 0)[1], 0, unroll=unroll)
    def tr(j):
        kt_ref[j] = tile(k_ref, j).T
        vt_ref[j] = tile(v_ref, j).T
    if True:
        loop(TILES, tr, 4)
    if True:
        loop(TILES, lambda i: fwd_tile(i, q_ref, k_ref, vt_ref, keys_ref, bias_ref, p_ref, s_ref, inv_ref, attn_ref), 4)
    if True:
        loop(TILES, lambda i: scale_rows(i, do_ref, inv_ref, dos_ref), 4)
        text_keys(p_ref, dos_ref, text_ref)
    if True:
        loop(TILES, lambda j: key_tile(j, keys_ref, pidx_ref, tsel_ref, p_ref, dos_ref, text_ref, dv_ref), 4)
    if True:
        loop(TILES, lambda i: bwd_tile(i, v_ref, kt_ref, do_ref, attn_ref, keys_ref, p_ref, inv_ref, dq_ref), 4)
    if True:
        text_keys(p_ref, q_ref, text_ref)
    if True:
        loop(TILES, lambda j: key_tile(j, keys_ref, pidx_ref, tsel_ref, p_ref, q_ref, text_ref, dk_ref), 4)

def attention(tabs, q, k, v, do):
    n = TILES * TILE
    V = pl.BlockSpec(memory_space=pltpu.VMEM); S = pl.BlockSpec(memory_space=pltpu.SMEM)
    return pl.pallas_call(attn_kernel,
        out_shape=[jax.ShapeDtypeStruct((n, HD), BF)] * 4,
        in_specs=[S]*4 + [V]*4, out_specs=[V]*4,
        scratch_shapes=[pltpu.VMEM((TILES*SLOTS+1, TILE, TILE), BF), pltpu.VMEM((SLOTS, TILE, TILE), F32),
            pltpu.VMEM((TILES, TILE, TILE), BF), pltpu.VMEM((TILES, TILE, TILE), BF), pltpu.VMEM((TILES, 1, TILE), F32),
            pltpu.VMEM((TXT+1, TILE, TILE), F32), pltpu.VMEM((n, HD), BF)],
        compiler_params=pltpu.CompilerParams(vmem_limit_bytes=60<<20), name="attention_core",
        )(*tabs, q, k, v, do)


def local(queries, key_states, value_states, residual, upstream, mod_gate, out_bias, w_out, neighbours, counts, text_tiles):
    def to_heads(x):
        return lax.all_to_all(x, "seq", split_axis=1, concat_axis=0, tiled=True)

    def to_tokens(x):
        return lax.all_to_all(x, "seq", split_axis=0, concat_axis=1, tiled=True)

    w = lax.all_gather(w_out, "fsdp", axis=0, tiled=True)
    tabs = tables(neighbours, counts, text_tiles)
    q, k, v = to_heads(queries[0]), to_heads(key_states[0]), to_heads(value_states[0])
    scaled = (upstream[0].astype(F32) * mod_gate[0][None, :]).astype(BF)
    d_attn = dot(scaled, w, NT).astype(BF)
    do = to_heads(d_attn)
    attn, dq, dk, dv = attention(tabs, q, k, v, do)
    attn, dq, dk, dv = [to_tokens(x) for x in (attn, dq, dk, dv)]
    projected = dot(attn, w)
    block_out = (residual[0].astype(F32) + mod_gate[0][None, :] * (projected + out_bias[None, :])).astype(BF)
    return block_out[None], dq[None], dk[None], dv[None]


def solution(mesh):
    act = P("fsdp", "seq", None)
    return jax.shard_map(local, mesh=mesh, in_specs=(act,) * 5 + (P("fsdp", None), P(), P("fsdp", None), P(), P(), P()),
                         out_specs=(act,) * 4, check_vma=False)
```

```python
import math
import jax, jax.numpy as jnp
from jax import lax
from jax.experimental import pallas as pl
from jax.experimental.pallas import tpu as pltpu
from jax.sharding import PartitionSpec as P

HD=128; TILE=128; TILES=48; NBR=9; TXT=4; SLOTS=13; D=3072; SEQ=6144; HDT=2048
FACTOR = 1.0/math.sqrt(HD)
EXP2 = FACTOR*math.log2(math.e)
F32=jnp.float32; BF=jnp.bfloat16

def table_kernel(text_ref, near_ref, near_t_ref, count_ref, count_t_ref, keys_ref, bias_ref, pidx_ref, tsel_ref):
    near, near_t, count, count_t = near_ref[...], near_t_ref[...], count_ref[...], count_t_ref[...]
    live = lax.broadcasted_iota(jnp.int32, (TILES, NBR), 1) < count
    keys_ref[:, :NBR] = jnp.where(live, near, near[:, :1])
    bias_ref[...] = jnp.where(live, 0.0, -jnp.inf).astype(F32)
    query = lax.broadcasted_iota(jnp.int32, (TILES, TILES), 0)
    key = lax.broadcasted_iota(jnp.int32, (TILES, TILES), 1)
    block = jnp.zeros((TILES, TILES), jnp.int32)
    for s in range(NBR):
        block = jnp.where((near[:, s:s + 1] == key) & (s < count), query * SLOTS + s + 1, block)
    ids = lax.broadcasted_iota(jnp.int32, (1, TILES), 1)
    tsel = jnp.full((1, TILES), TXT, jnp.int32)
    for u in range(TXT):
        keys_ref[:, NBR + u:NBR + u + 1] = jnp.full((TILES, 1), text_ref[u], jnp.int32)
        tsel = jnp.where(ids == text_ref[u], u, tsel)
    tsel_ref[...] = tsel
    for r in range(SLOTS):
        who = near_t[r:r + 1, :] if r < NBR else jnp.full((1, TILES), text_ref[r - NBR], jnp.int32)
        pick = jnp.sum(jnp.where(query == who, block, 0), axis=0, keepdims=True)
        ok = (pick > 0) & (tsel == TXT)
        if r < NBR:
            ok = ok & (r < count_t)
        pidx_ref[r:r + 1, :] = jnp.where(ok, pick - 1, TILES * SLOTS)


def tables(neighbours, counts, text_tiles):
    S, V = [pl.BlockSpec(memory_space=m) for m in (pltpu.SMEM, pltpu.VMEM)]
    i32 = jnp.int32
    return pl.pallas_call(
        table_kernel,
        out_shape=[jax.ShapeDtypeStruct((TILES, SLOTS), i32), jax.ShapeDtypeStruct((TILES, NBR), F32),
                   jax.ShapeDtypeStruct((SLOTS, TILES), i32), jax.ShapeDtypeStruct((1, TILES), i32)],
        in_specs=[S] + [V] * 4, out_specs=[V] * 4, name="tables",
    )(text_tiles, neighbours, neighbours.T, counts[:, None], counts[None, :])


def tile(ref, i):
    return ref[i]

NT = (((1,), (1,)), ((), ()))
NN = (((1,), (0,)), ((), ()))

def dot(a, b, dims=NN):
    return lax.dot_general(a, b, dims, preferred_element_type=F32)

def fwd_tile(i, q_ref, k_ref, vt_ref, keys_ref, bias_ref, p_ref, s_ref, inv_ref, attn_ref):
    q = tile(q_ref, i)
    top = None
    kc = jnp.concatenate([tile(k_ref, keys_ref[i, s]) for s in range(SLOTS)], axis=0)
    sall = dot(kc, q, NT).reshape(SLOTS, TILE, TILE)
    for s in range(SLOTS):
        sc = sall[s]
        s_ref[s] = sc
        top = sc if top is None else jnp.maximum(top, sc)
    m = jnp.max(top, axis=0, keepdims=True) * EXP2
    total = None
    parts = []
    for s in range(SLOTS):
        shift = m if s < 3 or s >= NBR else m - bias_ref[i, s]
        e = jnp.exp2(s_ref[s] * EXP2 - shift)
        total = e if total is None else total + e
        e16 = e.astype(BF)
        p_ref[i * SLOTS + s] = e16
        parts.append(e16)
    inv = 1.0 / jnp.sum(total, axis=0, keepdims=True)
    inv_ref[i] = inv
    pt = jnp.concatenate(parts, axis=0)
    vt = jnp.concatenate([vt_ref[keys_ref[i, s]] for s in range(SLOTS)], axis=1)
    attn_t = dot(vt, pt) * inv
    attn_ref[i] = attn_t.astype(BF).T

def key_tile(j, who_ref, pidx_ref, tsel_ref, p_ref, x_ref, text_ref, out_ref):
    lhs = jnp.concatenate([p_ref[pidx_ref[r, j]] for r in range(SLOTS)], axis=1)
    rhs = jnp.concatenate([tile(x_ref, who_ref[j, r]) for r in range(SLOTS)], axis=0)
    acc = dot(lhs, rhs) + text_ref[tsel_ref[0, j]]
    out_ref[j] = acc.astype(BF)

def text_keys(p_ref, x_ref, text_ref):
    G = 12
    text_ref[...] = jnp.zeros_like(text_ref)
    def body(g, _):
        rhs = x_ref[pl.ds(g * G, G)].reshape(G * TILE, HD)
        for u in range(TXT):
            lhs = jnp.concatenate([p_ref[(g * G + n) * SLOTS + NBR + u] for n in range(G)], axis=1)
            text_ref[u] += dot(lhs, rhs)
        return 0
    lax.fori_loop(0, TILES // G, body, 0)

def bwd_tile(i, v_ref, kt_ref, do_ref, attn_ref, keys_ref, p_ref, inv_ref, dq_ref):
    do = tile(do_ref, i)
    prod = do.astype(F32) * tile(attn_ref, i).astype(F32)
    delta = jnp.sum(prod.T, axis=0, keepdims=True)
    c = inv_ref[i] * FACTOR
    dc = delta * c
    vc = jnp.concatenate([tile(v_ref, keys_ref[i, s]) for s in range(SLOTS)], axis=0)
    dpall = dot(vc, do, NT).reshape(SLOTS, TILE, TILE)
    parts = [(p_ref[i * SLOTS + s].astype(F32) * (dpall[s] * c - dc)).astype(BF) for s in range(SLOTS)]
    for s in range(SLOTS): p_ref[i * SLOTS + s] = parts[s]
    ds = jnp.concatenate(parts, axis=0)
    kt = jnp.concatenate([kt_ref[keys_ref[i, s]] for s in range(SLOTS)], axis=1)
    dq_t = dot(kt, ds)
    dq_ref[i] = dq_t.astype(BF).T

def scale_rows(i, do_ref, inv_ref, dos_ref):
    col = jnp.broadcast_to(inv_ref[i], (TILE, TILE)).T
    dos_ref[i] = (do_ref[i].astype(F32) * col).astype(BF)


MESH = pl.DeviceIdType.MESH
PEERS = 16
ROWS = SEQ // PEERS
SHARD = 256
OWN = TILES // PEERS
K_, V_, Q_, O_, AT_, DV_, DQ_, DK_ = range(8)


def rows_of(p):
    return pl.ds(p * OWN, OWN)


def head_of(p):
    return pl.ds(pl.multiple_of(p * HD, HD), HD)


def block_kernel(keys_ref, bias_ref, pidx_ref, tsel_ref, gate_ref, obias_ref,
                 q_in, k_in, v_in, res_in, up_in, w_in,
                 out_ref, dq_out, dk_out, dv_out,
                 q_ref, k_ref, v_ref, do_ref, at_land, w_ref, up_ref, sc_ref, dst_ref,
                 at_st, dv_st, dq_st, dk_st,
                 p_ref, s_ref, kt_ref, vt_ref, inv_ref, text_ref,
                 send, recv, own, wsend, wrecv, lsem):
    me = lax.axis_index("seq")
    mx, mz = me // 4, me % 4
    f = lax.axis_index("fsdp")
    y, c = f // 2, f % 2
    sib = y * 2 + (1 - c)
    yup = ((y + 1) % 4) * 2 + c
    ydn = ((y + 3) % 4) * 2 + c
    far = ((y + 2) % 4) * 2 + c

    def peer(n):
        return ((mx + n // 4) % 4) * 4 + (mz + n % 4) % 4

    def loop(n, body, lo=0):
        lax.fori_loop(lo, n, lambda i, _: (body(i), 0)[1], 0)

    def wrows(shard, off=0, n=SHARD):
        return pl.ds(pl.multiple_of(shard * SHARD + off, 128), n)

    def to_head(a, src, land, p):
        return pltpu.make_async_remote_copy(src.at[:, :, head_of(p)], land.at[rows_of(me)], send.at[a, p], recv.at[a, me],
                                            device_id={"seq": p}, device_id_type=MESH)

    def to_rows(a, src, land, p):
        return pltpu.make_async_remote_copy(src.at[rows_of(p)], land.at[:, :, head_of(me)], send.at[a, p], recv.at[a, me],
                                            device_id={"seq": p}, device_id_type=MESH)

    def got_head(a, src, land, p):
        pltpu.make_async_remote_copy(src.at[:, :, head_of(p)], land.at[rows_of(p)], send.at[a, p], recv.at[a, p],
                                     device_id={"seq": p}, device_id_type=MESH).wait_recv()

    def got_rows(a, src, land, p):
        pltpu.make_async_remote_copy(src.at[rows_of(p)], land.at[:, :, head_of(p)], send.at[a, p], recv.at[a, p],
                                     device_id={"seq": p}, device_id_type=MESH).wait_recv()

    def own_head(a, src, land):
        return pltpu.make_async_copy(src.at[:, :, head_of(me)], land.at[rows_of(me)], own.at[a])

    def own_rows(a, src, land):
        return pltpu.make_async_copy(src.at[rows_of(me)], land.at[:, :, head_of(me)], own.at[a])

    def wcopy(k, shard, target, src=None, off=0, n=SHARD):
        part = w_ref.at[wrows(shard, off, n)]
        return pltpu.make_async_remote_copy(part if src is None else src, part, wsend.at[k], wrecv.at[k],
                                            device_id={"fsdp": target}, device_id_type=MESH)

    get_up = pltpu.make_async_copy(up_in, up_ref, lsem.at[0])
    get_up.start()
    get_w = pltpu.make_async_copy(w_in, w_ref.at[wrows(f)], lsem.at[1])
    get_w.start()

    barrier = pltpu.get_barrier_semaphore()
    loop(PEERS, lambda n: pl.semaphore_signal(barrier, inc=1, device_id={"seq": peer(n)}, device_id_type=MESH), 1)
    for t in (sib, yup, ydn):
        pl.semaphore_signal(barrier, inc=1, device_id={"fsdp": t}, device_id_type=MESH)
    pl.semaphore_wait(barrier, PEERS + 2)

    w_up = wcopy(0, f, yup, w_in)
    w_dn = wcopy(1, f, ydn, w_in)
    w_sib = wcopy(4, f, sib, w_in)
    w_up.start()
    w_dn.start()
    w_sib.start()
    for a, src, land in ((K_, k_in, k_ref), (V_, v_in, v_ref), (Q_, q_in, q_ref)):
        own_head(a, src, land).start()
        loop(PEERS, lambda n, a=a, src=src, land=land: to_head(a, src, land, peer(n)).start(), 1)

    p_ref[TILES * SLOTS] = jnp.zeros((TILE, TILE), BF)
    get_up.wait()

    def scale_up(g):
        sl = pl.ds(pl.multiple_of(g * 32, 32), 32)
        sc_ref[sl, :] = (up_ref[sl, :].astype(F32) * gate_ref[...]).astype(BF)

    loop(ROWS // 32, scale_up)
    get_res = pltpu.make_async_copy(res_in, up_ref, lsem.at[0])
    get_res.start()

    def d_attn(shard):
        r = dot(sc_ref[...], w_ref[wrows(shard), :], NT).astype(BF)
        dst_ref[:, :, pl.ds(pl.multiple_of(shard * SHARD, SHARD), SHARD)] = r.reshape(OWN, TILE, SHARD)

    get_w.wait()
    d_attn(f)
    w_sib.wait_recv()
    d_attn(sib)

    def turn(src, dst):
        def body(n):
            p = peer(n)
            for t in range(3):
                dst[p * 3 + t] = tile(src, p * 3 + t).T
        return body

    own_head(K_, k_in, k_ref).wait()
    loop(PEERS, lambda n: got_head(K_, k_in, k_ref, peer(n)), 1)
    loop(PEERS, turn(k_ref, kt_ref))
    w_up.wait_recv()
    fwd_up = wcopy(2, ydn, yup, None, 0, 128)
    fwd_up.start()
    sh_dn = wcopy(5, ydn, sib)
    sh_dn.start()
    w_dn.wait_recv()
    fwd_dn = wcopy(3, yup, ydn, None, 128, 128)
    fwd_dn.start()
    sh_up = wcopy(6, yup, sib)
    sh_up.start()
    d_attn(ydn)
    d_attn(yup)
    own_head(V_, v_in, v_ref).wait()
    loop(PEERS, lambda n: got_head(V_, v_in, v_ref, peer(n)), 1)
    loop(PEERS, turn(v_ref, vt_ref))
    sh_dn.wait_recv()
    d_attn(ydn + 1 - 2 * c)
    sh_up.wait_recv()
    d_attn(yup + 1 - 2 * c)
    wcopy(2, far, yup, None, 0, 128).wait_recv()
    wcopy(3, far, yup, None, 128, 128).wait_recv()
    sh_far = wcopy(7, far, sib)
    sh_far.start()
    d_attn(far)
    own_head(Q_, q_in, q_ref).wait()
    loop(PEERS, lambda n: got_head(Q_, q_in, q_ref, peer(n)), 1)
    sh_far.wait_recv()
    d_attn(far + 1 - 2 * c)
    own_head(O_, dst_ref, do_ref).start()
    loop(PEERS, lambda n: to_head(O_, dst_ref, do_ref, peer(n)).start(), 1)

    def stage(a, st, land, per_tile):
        def body(n):
            p = peer(n)
            for t in range(3):
                per_tile(p * 3 + t)

            @pl.when(n < PEERS)
            def _():
                to_rows(a, st, land, p).start()

        loop(PEERS + 1, body, 1)
        own_rows(a, st, land).start()

    stage(AT_, at_st, at_land, lambda i: fwd_tile(i, q_ref, k_ref, vt_ref, keys_ref, bias_ref, p_ref, s_ref, inv_ref, at_st))
    own_head(O_, dst_ref, do_ref).wait()
    loop(PEERS, lambda n: got_head(O_, dst_ref, do_ref, peer(n)), 1)
    lax.fori_loop(0, TILES, lambda i, _: (scale_rows(i, do_ref, inv_ref, dq_st), 0)[1], 0, unroll=4)
    text_keys(p_ref, dq_st, text_ref)
    stage(DV_, dv_st, dv_out, lambda j: key_tile(j, keys_ref, pidx_ref, tsel_ref, p_ref, dq_st, text_ref, dv_st))
    stage(DQ_, dq_st, dq_out, lambda i: bwd_tile(i, v_ref, kt_ref, do_ref, at_st, keys_ref, p_ref, inv_ref, dq_st))
    text_keys(p_ref, q_ref, text_ref)
    stage(DK_, dk_st, dk_out, lambda j: key_tile(j, keys_ref, pidx_ref, tsel_ref, p_ref, q_ref, text_ref, dk_st))

    own_rows(AT_, at_st, at_land).wait()
    loop(PEERS, lambda n: got_rows(AT_, at_st, at_land, peer(n)), 1)
    get_res.wait()

    def project(g):
        sl = pl.ds(pl.multiple_of(g * 256, 256), 256)
        acc = dot(at_land[...].reshape(ROWS, HDT), w_ref[:, sl]) + obias_ref[:, sl]
        sc_ref[:, sl] = (up_ref[:, sl].astype(F32) + gate_ref[:, sl] * acc).astype(BF)

    loop(D // 256, project)
    put = pltpu.make_async_copy(sc_ref, out_ref, lsem.at[1])
    put.start()

    outs = ((DV_, dv_st, dv_out), (DQ_, dq_st, dq_out), (DK_, dk_st, dk_out))
    for a, st, land in outs:
        own_rows(a, st, land).wait()
        loop(PEERS, lambda n, a=a, st=st, land=land: got_rows(a, st, land, peer(n)), 1)
    for cp in (w_up, w_dn, w_sib, fwd_up, fwd_dn, sh_dn, sh_up, sh_far):
        cp.wait_send()
    for a, src, land in ((K_, k_in, k_ref), (V_, v_in, v_ref), (Q_, q_in, q_ref), (O_, dst_ref, do_ref)):
        loop(PEERS, lambda n, a=a, src=src, land=land: to_head(a, src, land, peer(n)).wait_send(), 1)
    for a, st, land in ((AT_, at_st, at_land),) + outs:
        loop(PEERS, lambda n, a=a, st=st, land=land: to_rows(a, st, land, peer(n)).wait_send(), 1)
    put.wait()


def local(queries, key_states, value_states, residual, upstream, mod_gate, out_bias, w_out, neighbours, counts, text_tiles):
    tabs = tables(neighbours, counts, text_tiles)
    S, V, A = [pl.BlockSpec(memory_space=m) for m in (pltpu.SMEM, pltpu.VMEM, pl.ANY)]
    head = pltpu.VMEM((TILES, TILE, HD), BF)
    tok = pltpu.VMEM((ROWS, D), BF)
    mid = pltpu.VMEM((OWN, TILE, HDT), BF)
    dma = pltpu.SemaphoreType.DMA
    act = jax.ShapeDtypeStruct((OWN, TILE, HDT), BF)
    out, dq, dk, dv = pl.pallas_call(
        block_kernel,
        out_shape=[jax.ShapeDtypeStruct((ROWS, D), BF), act, act, act],
        in_specs=[S] * 4 + [V] * 2 + [A] * 6,
        out_specs=[A] * 4,
        scratch_shapes=[head, head, head, head, mid, pltpu.VMEM((HDT, D), BF), tok, tok, mid,
                        head, head, head, head,
                        pltpu.VMEM((TILES * SLOTS + 1, TILE, TILE), BF), pltpu.VMEM((SLOTS, TILE, TILE), F32),
                        pltpu.VMEM((TILES, TILE, TILE), BF), pltpu.VMEM((TILES, TILE, TILE), BF),
                        pltpu.VMEM((TILES, 1, TILE), F32), pltpu.VMEM((TXT + 1, TILE, TILE), F32),
                        dma((8, PEERS)), dma((8, PEERS)), dma((8,)), dma((8,)), dma((8,)), dma((2,))],
        compiler_params=pltpu.CompilerParams(collective_id=0, has_side_effects=True, vmem_limit_bytes=60 << 20),
        name="attention_block",
    )(*tabs, mod_gate, out_bias[None, :],
      *[x.reshape(OWN, TILE, HDT) for x in (queries, key_states, value_states)], residual[0], upstream[0], w_out)
    return (out[None], *[x.reshape(1, ROWS, HDT) for x in (dq, dk, dv)])


def solution(mesh):
    act = P("fsdp", "seq", None)
    return jax.shard_map(local, mesh=mesh, in_specs=(act,) * 5 + (P("fsdp", None), P(), P("fsdp", None), P(), P(), P()),
                         out_specs=(act,) * 4, check_vma=False)
```

```python
import math
import jax, jax.numpy as jnp
from jax import lax
from jax.experimental import pallas as pl
from jax.experimental.pallas import tpu as pltpu
from jax.sharding import PartitionSpec as P

HD=128; TILE=128; TILES=48; NBR=9; TXT=4; SLOTS=13; D=3072; SEQ=6144; HDT=2048
FACTOR = 1.0/math.sqrt(HD)
EXP2 = FACTOR*math.log2(math.e)
F32=jnp.float32; BF=jnp.bfloat16

def fill_tables(text, near_ref, count_ref, pad_ref, keys_ref, bias_ref, pidx_ref, tsel_ref):
    pad_ref[...] = jnp.zeros((TILE, TILE), jnp.int32)
    pad_ref[:TILES, :NBR] = near_ref[...]
    near, near_t = pad_ref[:TILES, :NBR], pad_ref[...].T[:NBR, :TILES]
    count_t = count_ref[...]
    pad_ref[:1, :TILES] = count_t
    count = pad_ref[...].T[:TILES, :1]
    query = lax.broadcasted_iota(jnp.int32, (TILES, TILES), 0)
    key = lax.broadcasted_iota(jnp.int32, (TILES, TILES), 1)
    block = jnp.zeros((TILES, TILES), jnp.int32)
    for s in range(NBR):
        block = jnp.where((near[:, s:s + 1] == key) & (s < count), query * SLOTS + s + 1, block)
    ids = lax.broadcasted_iota(jnp.int32, (1, TILES), 1)
    tsel = jnp.full((1, TILES), TXT, jnp.int32)
    for u in range(TXT):
        tsel = jnp.where(ids == text[u], u, tsel)
    tsel_ref[:1, :TILES] = tsel
    for r in range(SLOTS):
        live = r < count_t
        if r < NBR:
            who = near_t[r:r + 1, :]
            keys_ref[r:r + 1, :TILES] = jnp.where(live, who, near_t[:1, :])
            bias_ref[r:r + 1, :TILES] = jnp.where(live, 0.0, -jnp.inf).astype(F32)
        else:
            who = jnp.full((1, TILES), text[r - NBR], jnp.int32)
            keys_ref[r:r + 1, :TILES] = who
        pick = jnp.sum(jnp.where(query == who, block, 0), axis=0, keepdims=True)
        ok = (pick > 0) & (tsel == TXT)
        if r < NBR:
            ok = ok & live
        pidx_ref[r:r + 1, :TILES] = jnp.where(ok, pick - 1, TILES * SLOTS)


def tile(ref, i):
    return ref[i]

NT = (((1,), (1,)), ((), ()))
NN = (((1,), (0,)), ((), ()))

def dot(a, b, dims=NN):
    return lax.dot_general(a, b, dims, preferred_element_type=F32)

def fwd_tile(i, q_ref, k_ref, vt_ref, keys_ref, bias_ref, p_ref, s_ref, inv_ref, attn_ref):
    q = tile(q_ref, i)
    top = None
    kc = jnp.concatenate([tile(k_ref, keys_ref[s, i]) for s in range(SLOTS)], axis=0)
    sall = dot(kc, q, NT).reshape(SLOTS, TILE, TILE)
    for s in range(SLOTS):
        sc = sall[s]
        s_ref[s] = sc
        top = sc if top is None else jnp.maximum(top, sc)
    m = jnp.max(top, axis=0, keepdims=True) * EXP2
    total = None
    parts = []
    for s in range(SLOTS):
        shift = m if s < 3 or s >= NBR else m - bias_ref[s, i]
        e = jnp.exp2(s_ref[s] * EXP2 - shift)
        total = e if total is None else total + e
        e16 = e.astype(BF)
        p_ref[i * SLOTS + s] = e16
        parts.append(e16)
    inv = 1.0 / jnp.sum(total, axis=0, keepdims=True)
    inv_ref[i] = inv
    pt = jnp.concatenate(parts, axis=0)
    vt = jnp.concatenate([vt_ref[keys_ref[s, i]] for s in range(SLOTS)], axis=1)
    attn_t = dot(vt, pt) * inv
    attn_ref[i] = attn_t.astype(BF).T

def key_tile(j, who_ref, pidx_ref, tsel_ref, p_ref, x_ref, text_ref, out_ref):
    lhs = jnp.concatenate([p_ref[pidx_ref[r, j]] for r in range(SLOTS)], axis=1)
    rhs = jnp.concatenate([tile(x_ref, who_ref[r, j]) for r in range(SLOTS)], axis=0)
    acc = dot(lhs, rhs) + text_ref[tsel_ref[0, j]]
    out_ref[j] = acc.astype(BF)

def text_keys(p_ref, x_ref, text_ref):
    G = 12
    text_ref[...] = jnp.zeros_like(text_ref)
    def body(g, _):
        rhs = x_ref[pl.ds(g * G, G)].reshape(G * TILE, HD)
        for u in range(TXT):
            lhs = jnp.concatenate([p_ref[(g * G + n) * SLOTS + NBR + u] for n in range(G)], axis=1)
            text_ref[u] += dot(lhs, rhs)
        return 0
    lax.fori_loop(0, TILES // G, body, 0)

def bwd_tile(i, v_ref, kt_ref, do_ref, attn_ref, keys_ref, p_ref, inv_ref, dq_ref):
    do = tile(do_ref, i)
    prod = do.astype(F32) * tile(attn_ref, i).astype(F32)
    delta = jnp.sum(prod.T, axis=0, keepdims=True)
    c = inv_ref[i] * FACTOR
    dc = delta * c
    vc = jnp.concatenate([tile(v_ref, keys_ref[s, i]) for s in range(SLOTS)], axis=0)
    dpall = dot(vc, do, NT).reshape(SLOTS, TILE, TILE)
    parts = [(p_ref[i * SLOTS + s].astype(F32) * (dpall[s] * c - dc)).astype(BF) for s in range(SLOTS)]
    for s in range(SLOTS): p_ref[i * SLOTS + s] = parts[s]
    ds = jnp.concatenate(parts, axis=0)
    kt = jnp.concatenate([kt_ref[keys_ref[s, i]] for s in range(SLOTS)], axis=1)
    dq_t = dot(kt, ds)
    dq_ref[i] = dq_t.astype(BF).T

def scale_rows(i, do_ref, inv_ref, dos_ref):
    col = jnp.broadcast_to(inv_ref[i], (TILE, TILE)).T
    dos_ref[i] = (do_ref[i].astype(F32) * col).astype(BF)


MESH = pl.DeviceIdType.MESH
PEERS = 16
ROWS = SEQ // PEERS
SHARD = 256
OWN = TILES // PEERS
K_, V_, Q_, O_, AT_, DV_, DQ_, DK_ = range(8)


def rows_of(p):
    return pl.ds(p * OWN, OWN)


def head_of(p):
    return pl.ds(pl.multiple_of(p * HD, HD), HD)


def block_kernel(text_tiles, near_ref, count_ref, gate_ref, obias_ref,
                 q_in, k_in, v_in, res_in, up_in, w_in,
                 sc_ref, dq_out, dk_out, dv_out,
                 q_ref, k_ref, v_ref, do_ref, at_land, w_ref, up_ref, dst_ref,
                 at_st, dq_st,
                 p_ref, s_ref, kt_ref, vt_ref, inv_ref, text_ref,
                 keys_ref, bias_ref, pidx_ref, tsel_ref, keys_v, bias_v, pidx_v, tsel_v, pad_ref,
                 send, recv, own, wsend, wrecv, lsem):
    me = lax.axis_index("seq")
    mx, mz = me // 4, me % 4
    f = lax.axis_index("fsdp")
    y, c = f // 2, f % 2
    sib = y * 2 + (1 - c)
    yup = ((y + 1) % 4) * 2 + c
    ydn = ((y + 3) % 4) * 2 + c
    far = ((y + 2) % 4) * 2 + c

    def peer(n):
        n = (n * 7) % PEERS
        return ((mx + n // 4) % 4) * 4 + (mz + n % 4) % 4

    def loop(n, body, lo=0):
        lax.fori_loop(lo, n, lambda i, _: (body(i), 0)[1], 0)

    def wrows(shard, off=0, n=SHARD):
        return pl.ds(pl.multiple_of(shard * SHARD + off, 128), n)

    def to_head(a, src, land, p):
        return pltpu.make_async_remote_copy(src.at[:, :, head_of(p)], land.at[rows_of(me)], send.at[a, p], recv.at[a, me],
                                            device_id={"seq": p}, device_id_type=MESH)

    def to_rows(a, src, land, p):
        return pltpu.make_async_remote_copy(src.at[rows_of(p)], land.at[:, :, head_of(me)], send.at[a, p], recv.at[a, me],
                                            device_id={"seq": p}, device_id_type=MESH)

    def got_head(a, src, land, p):
        pltpu.make_async_remote_copy(src.at[:, :, head_of(p)], land.at[rows_of(p)], send.at[a, p], recv.at[a, p],
                                     device_id={"seq": p}, device_id_type=MESH).wait_recv()

    def got_rows(a, src, land, p):
        pltpu.make_async_remote_copy(src.at[rows_of(p)], land.at[:, :, head_of(p)], send.at[a, p], recv.at[a, p],
                                     device_id={"seq": p}, device_id_type=MESH).wait_recv()

    def own_head(a, src, land):
        return pltpu.make_async_copy(src.at[:, :, head_of(me)], land.at[rows_of(me)], own.at[a])

    def own_rows(a, src, land):
        return pltpu.make_async_copy(src.at[rows_of(me)], land.at[:, :, head_of(me)], own.at[a])

    def wcopy(k, shard, target, src=None, off=0, n=SHARD):
        part = w_ref.at[wrows(shard, off, n)]
        return pltpu.make_async_remote_copy(part if src is None else src, part, wsend.at[k], wrecv.at[k],
                                            device_id={"fsdp": target}, device_id_type=MESH)

    dv_st, dk_st = k_ref, do_ref

    get_up = pltpu.make_async_copy(up_in, up_ref, lsem.at[0])
    get_up.start()
    get_w = pltpu.make_async_copy(w_in, w_ref.at[wrows(f)], lsem.at[1])
    get_w.start()

    barrier = pltpu.get_barrier_semaphore()
    loop(PEERS, lambda n: pl.semaphore_signal(barrier, inc=1, device_id={"seq": peer(n)}, device_id_type=MESH), 1)
    for t in (sib, yup, ydn):
        pl.semaphore_signal(barrier, inc=1, device_id={"fsdp": t}, device_id_type=MESH)
    pl.semaphore_wait(barrier, PEERS + 2)

    w_up = wcopy(0, f, yup, w_in)
    w_dn = wcopy(1, f, ydn, w_in)
    w_sib = wcopy(4, f, sib, w_in)
    w_up.start()
    w_dn.start()
    w_sib.start()
    for a, src, land in ((K_, k_in, k_ref), (V_, v_in, v_ref), (Q_, q_in, q_ref)):
        own_head(a, src, land).start()
        loop(PEERS, lambda n, a=a, src=src, land=land: to_head(a, src, land, peer(n)).start(), 1)

    fill_tables([text_tiles[u] for u in range(TXT)], near_ref, count_ref, pad_ref, keys_v, bias_v, pidx_v, tsel_v)
    moves = [pltpu.make_async_copy(a, b, lsem.at[2 + k]) for k, (a, b) in enumerate(
        ((keys_v, keys_ref), (bias_v, bias_ref), (pidx_v, pidx_ref), (tsel_v, tsel_ref)))]
    for move in moves:
        move.start()
    p_ref[TILES * SLOTS] = jnp.zeros((TILE, TILE), BF)
    get_up.wait()

    def scale_up(g):
        sl = pl.ds(pl.multiple_of(g * 32, 32), 32)
        sc_ref[sl, :] = (up_ref[sl, :].astype(F32) * gate_ref[...]).astype(BF)

    loop(ROWS // 32, scale_up)
    get_res = pltpu.make_async_copy(res_in, up_ref, lsem.at[0])
    get_res.start()

    def d_attn(shard):
        r = dot(sc_ref[...], w_ref[wrows(shard), :], NT).astype(BF)
        dst_ref[:, :, pl.ds(pl.multiple_of(shard * SHARD, SHARD), SHARD)] = r.reshape(OWN, TILE, SHARD)

    for move in moves:
        move.wait()
    get_w.wait()
    d_attn(f)
    w_sib.wait_recv()
    d_attn(sib)

    def turn(src, dst):
        def body(n):
            p = peer(n)
            for t in range(3):
                dst[p * 3 + t] = tile(src, p * 3 + t).T
        return body

    own_head(K_, k_in, k_ref).wait()
    loop(PEERS, lambda n: got_head(K_, k_in, k_ref, peer(n)), 1)
    loop(PEERS, turn(k_ref, kt_ref))
    w_up.wait_recv()
    fwd_up = wcopy(2, ydn, yup, None, 0, 128)
    fwd_up.start()
    sh_dn = wcopy(5, ydn, sib)
    sh_dn.start()
    w_dn.wait_recv()
    fwd_dn = wcopy(3, yup, ydn, None, 128, 128)
    fwd_dn.start()
    sh_up = wcopy(6, yup, sib)
    sh_up.start()
    d_attn(ydn)
    d_attn(yup)
    own_head(V_, v_in, v_ref).wait()
    loop(PEERS, lambda n: got_head(V_, v_in, v_ref, peer(n)), 1)
    loop(PEERS, turn(v_ref, vt_ref))
    sh_dn.wait_recv()
    d_attn(ydn + 1 - 2 * c)
    sh_up.wait_recv()
    d_attn(yup + 1 - 2 * c)
    own_head(Q_, q_in, q_ref).wait()
    loop(PEERS, lambda n: got_head(Q_, q_in, q_ref, peer(n)), 1)

    def stage(a, st, land, per_tile, lo=1, hi=PEERS + 1):
        def body(n):
            p = peer(n)
            for t in range(3):
                per_tile(p * 3 + t)

            @pl.when(n < PEERS)
            def _():
                to_rows(a, st, land, p).start()

        loop(hi, body, lo)
        if hi > PEERS:
            own_rows(a, st, land).start()

    def forward(lo, hi):
        stage(AT_, at_st, at_land, lambda i: fwd_tile(i, q_ref, k_ref, vt_ref, keys_ref, bias_ref, p_ref, s_ref, inv_ref, at_st), lo, hi)

    forward(1, 4)
    wcopy(2, far, yup, None, 0, 128).wait_recv()
    wcopy(3, far, yup, None, 128, 128).wait_recv()
    sh_far = wcopy(7, far, sib)
    sh_far.start()
    forward(4, 7)
    d_attn(far)
    sh_far.wait_recv()
    d_attn(far + 1 - 2 * c)
    loop(PEERS, lambda n: to_head(O_, dst_ref, do_ref, peer(n)).start(), 1)
    own_head(O_, dst_ref, do_ref).start()
    forward(7, PEERS + 1)
    own_head(O_, dst_ref, do_ref).wait()
    loop(PEERS, lambda n: got_head(O_, dst_ref, do_ref, peer(n)), 1)
    lax.fori_loop(0, TILES, lambda i, _: (scale_rows(i, do_ref, inv_ref, dq_st), 0)[1], 0, unroll=4)
    text_keys(p_ref, dq_st, text_ref)
    stage(DV_, dv_st, dv_out, lambda j: key_tile(j, keys_ref, pidx_ref, tsel_ref, p_ref, dq_st, text_ref, dv_st))
    stage(DQ_, dq_st, dq_out, lambda i: bwd_tile(i, v_ref, kt_ref, do_ref, at_st, keys_ref, p_ref, inv_ref, dq_st))
    text_keys(p_ref, q_ref, text_ref)
    stage(DK_, dk_st, dk_out, lambda j: key_tile(j, keys_ref, pidx_ref, tsel_ref, p_ref, q_ref, text_ref, dk_st))

    own_rows(AT_, at_st, at_land).wait()
    loop(PEERS, lambda n: got_rows(AT_, at_st, at_land, peer(n)), 1)
    get_res.wait()

    def project(g):
        sl = pl.ds(pl.multiple_of(g * 256, 256), 256)
        acc = dot(at_land[...].reshape(ROWS, HDT), w_ref[:, sl]) + obias_ref[:, sl]
        sc_ref[:, sl] = (up_ref[:, sl].astype(F32) + gate_ref[:, sl] * acc).astype(BF)

    loop(D // 256, project)

    outs = ((DV_, dv_st, dv_out), (DQ_, dq_st, dq_out), (DK_, dk_st, dk_out))
    for a, st, land in outs:
        own_rows(a, st, land).wait()
        loop(PEERS, lambda n, a=a, st=st, land=land: got_rows(a, st, land, peer(n)), 1)
    for cp in (w_up, w_dn, w_sib, fwd_up, fwd_dn, sh_dn, sh_up, sh_far):
        cp.wait_send()
    for a, src, land in ((K_, k_in, k_ref), (V_, v_in, v_ref), (Q_, q_in, q_ref), (O_, dst_ref, do_ref)):
        loop(PEERS, lambda n, a=a, src=src, land=land: to_head(a, src, land, peer(n)).wait_send(), 1)
    for a, st, land in ((AT_, at_st, at_land),) + outs:
        loop(PEERS, lambda n, a=a, st=st, land=land: to_rows(a, st, land, peer(n)).wait_send(), 1)


def local(queries, key_states, value_states, residual, upstream, mod_gate, out_bias, w_out, neighbours, counts, text_tiles):
    S, V, A = [pl.BlockSpec(memory_space=m) for m in (pltpu.SMEM, pltpu.VMEM, pl.ANY)]
    head = pltpu.VMEM((TILES, TILE, HD), BF)
    tok = pltpu.VMEM((ROWS, D), BF)
    mid = pltpu.VMEM((OWN, TILE, HDT), BF)
    dma = pltpu.SemaphoreType.DMA
    i32 = jnp.int32
    act = jax.ShapeDtypeStruct((OWN, TILE, HDT), BF)
    out, dq, dk, dv = pl.pallas_call(
        block_kernel,
        out_shape=[tok, mid, mid, mid],
        in_specs=[S] + [V] * 4 + [A] * 6,
        out_specs=[V] * 4,
        scratch_shapes=[head, head, head, head, mid, pltpu.VMEM((HDT, D), BF), tok, mid,
                        head, head,
                        pltpu.VMEM((TILES * SLOTS + 1, TILE, TILE), BF), pltpu.VMEM((SLOTS, TILE, TILE), F32),
                        pltpu.VMEM((TILES, TILE, TILE), BF), pltpu.VMEM((TILES, TILE, TILE), BF),
                        pltpu.VMEM((TILES, 1, TILE), F32), pltpu.VMEM((TXT + 1, TILE, TILE), F32),
                        *[m((n, TILE), t) for m in (pltpu.SMEM, pltpu.VMEM) for n, t in ((16, i32), (16, F32), (16, i32), (8, i32))],
                        pltpu.VMEM((TILE, TILE), i32),
                        dma((8, PEERS)), dma((8, PEERS)), dma((8,)), dma((8,)), dma((8,)), dma((6,))],
        compiler_params=pltpu.CompilerParams(collective_id=0, has_side_effects=True, vmem_limit_bytes=54 << 20),
        name="attention_block",
    )(text_tiles, neighbours, counts[None, :], mod_gate, out_bias[None, :],
      *[x.reshape(OWN, TILE, HDT) for x in (queries, key_states, value_states)], residual[0], upstream[0], w_out)
    return (out[None], *[x.reshape(1, ROWS, HDT) for x in (dq, dk, dv)])


def solution(mesh):
    act = P("fsdp", "seq", None)
    return jax.shard_map(local, mesh=mesh, in_specs=(act,) * 5 + (P("fsdp", None), P(), P("fsdp", None), P(), P(), P()),
                         out_specs=(act,) * 4, check_vma=False)
```

```python
import math
import jax, jax.numpy as jnp
from jax import lax
from jax.experimental import pallas as pl
from jax.experimental.pallas import tpu as pltpu
from jax.sharding import PartitionSpec as P

HD=128; TILE=128; TILES=48; NBR=9; TXT=4; SLOTS=13; D=3072; SEQ=6144; HDT=2048
FACTOR = 1.0/math.sqrt(HD)
EXP2 = FACTOR*math.log2(math.e)
F32=jnp.float32; BF=jnp.bfloat16

def fill_tables(text, near_ref, count_ref, pad_ref, keys_ref, bias_ref, pidx_ref, tsel_ref):
    pad_ref[...] = jnp.zeros((TILE, TILE), jnp.int32)
    near_t = near_ref[...]
    pad_ref[:NBR, :TILES] = near_t
    near = pad_ref[...].T[:TILES, :NBR]
    count_t = count_ref[...]
    pad_ref[:1, :TILES] = count_t
    count = pad_ref[...].T[:TILES, :1]
    query = lax.broadcasted_iota(jnp.int32, (TILES, TILES), 0)
    key = lax.broadcasted_iota(jnp.int32, (TILES, TILES), 1)
    block = jnp.zeros((TILES, TILES), jnp.int32)
    for s in range(NBR):
        block = jnp.where((near[:, s:s + 1] == key) & (s < count), query * SLOTS + s + 1, block)
    ids = lax.broadcasted_iota(jnp.int32, (1, TILES), 1)
    tsel = jnp.full((1, TILES), TXT, jnp.int32)
    for u in range(TXT):
        tsel = jnp.where(ids == text[u], u, tsel)
    tsel_ref[:1, :TILES] = tsel
    for r in range(SLOTS):
        live = r < count_t
        if r < NBR:
            who = near_t[r:r + 1, :]
            keys_ref[r:r + 1, :TILES] = jnp.where(live, who, near_t[:1, :])
            bias_ref[r:r + 1, :TILES] = jnp.where(live, 0.0, -jnp.inf).astype(F32)
        else:
            who = jnp.full((1, TILES), text[r - NBR], jnp.int32)
            keys_ref[r:r + 1, :TILES] = who
        pick = jnp.sum(jnp.where(query == who, block, 0), axis=0, keepdims=True)
        ok = (pick > 0) & (tsel == TXT)
        if r < NBR:
            ok = ok & live
        pidx_ref[r:r + 1, :TILES] = jnp.where(ok, pick - 1, TILES * SLOTS)


def tile(ref, i):
    return ref[i]

NT = (((1,), (1,)), ((), ()))
NN = (((1,), (0,)), ((), ()))

def dot(a, b, dims=NN):
    return lax.dot_general(a, b, dims, preferred_element_type=F32)

def fwd_tile(i, q_ref, k_ref, vt_ref, keys_ref, bias_ref, p_ref, s_ref, inv_ref, attn_ref):
    q = tile(q_ref, i)
    top = None
    kc = jnp.concatenate([tile(k_ref, keys_ref[s, i]) for s in range(SLOTS)], axis=0)
    sall = dot(kc, q, NT).reshape(SLOTS, TILE, TILE)
    for s in range(SLOTS):
        sc = sall[s]
        s_ref[s] = sc
        top = sc if top is None else jnp.maximum(top, sc)
    m = jnp.max(top, axis=0, keepdims=True) * EXP2
    total = None
    parts = []
    for s in range(SLOTS):
        shift = m if s < 3 or s >= NBR else m - bias_ref[s, i]
        e = jnp.exp2(s_ref[s] * EXP2 - shift)
        total = e if total is None else total + e
        e16 = e.astype(BF)
        p_ref[i * SLOTS + s] = e16
        parts.append(e16)
    inv = 1.0 / jnp.sum(total, axis=0, keepdims=True)
    inv_ref[i] = inv
    pt = jnp.concatenate(parts, axis=0)
    vt = jnp.concatenate([vt_ref[keys_ref[s, i]] for s in range(SLOTS)], axis=1)
    attn_t = dot(vt, pt) * inv
    attn_ref[i] = attn_t.astype(BF).T

def key_tile(j, who_ref, pidx_ref, tsel_ref, p_ref, x_ref, text_ref, out_ref):
    lhs = jnp.concatenate([p_ref[pidx_ref[r, j]] for r in range(SLOTS)], axis=1)
    rhs = jnp.concatenate([tile(x_ref, who_ref[r, j]) for r in range(SLOTS)], axis=0)
    acc = dot(lhs, rhs) + text_ref[tsel_ref[0, j]]
    out_ref[j] = acc.astype(BF)

def text_keys(p_ref, x_ref, text_ref):
    G = 12
    text_ref[...] = jnp.zeros_like(text_ref)
    def body(g, _):
        rhs = x_ref[pl.ds(g * G, G)].reshape(G * TILE, HD)
        for u in range(TXT):
            lhs = jnp.concatenate([p_ref[(g * G + n) * SLOTS + NBR + u] for n in range(G)], axis=1)
            text_ref[u] += dot(lhs, rhs)
        return 0
    lax.fori_loop(0, TILES // G, body, 0)

def bwd_tile(i, v_ref, kt_ref, do_ref, attn_ref, keys_ref, p_ref, inv_ref, dq_ref):
    do = tile(do_ref, i)
    prod = do.astype(F32) * tile(attn_ref, i).astype(F32)
    delta = jnp.sum(prod.T, axis=0, keepdims=True)
    c = inv_ref[i] * FACTOR
    dc = delta * c
    vc = jnp.concatenate([tile(v_ref, keys_ref[s, i]) for s in range(SLOTS)], axis=0)
    dpall = dot(vc, do, NT).reshape(SLOTS, TILE, TILE)
    parts = [(p_ref[i * SLOTS + s].astype(F32) * (dpall[s] * c - dc)).astype(BF) for s in range(SLOTS)]
    for s in range(SLOTS): p_ref[i * SLOTS + s] = parts[s]
    ds = jnp.concatenate(parts, axis=0)
    kt = jnp.concatenate([kt_ref[keys_ref[s, i]] for s in range(SLOTS)], axis=1)
    dq_t = dot(kt, ds)
    dq_ref[i] = dq_t.astype(BF).T

def scale_rows(i, do_ref, inv_ref, dos_ref):
    col = jnp.broadcast_to(inv_ref[i], (TILE, TILE)).T
    dos_ref[i] = (do_ref[i].astype(F32) * col).astype(BF)


MESH = pl.DeviceIdType.MESH
PEERS = 16
ROWS = SEQ // PEERS
SHARD = 256
OWN = TILES // PEERS
K_, V_, Q_, O_, AT_, DV_, DQ_, DK_ = range(8)


def rows_of(p):
    return pl.ds(p * OWN, OWN)


def head_of(p):
    return pl.ds(pl.multiple_of(p * HD, HD), HD)


def block_kernel(text_tiles, near_ref, count_ref, gate_ref, obias_ref,
                 q_in, k_in, v_in, res_in, up_in, w_in,
                 sc_ref, dq_out, dk_out, dv_out,
                 q_ref, k_ref, v_ref, do_ref, at_land, w_ref, up_ref, dst_ref,
                 at_st, dq_st,
                 p_ref, s_ref, kt_ref, vt_ref, inv_ref, text_ref,
                 keys_ref, bias_ref, pidx_ref, tsel_ref, keys_v, bias_v, pidx_v, tsel_v, pad_ref,
                 send, recv, own, wsend, wrecv, lsem):
    me = lax.axis_index("seq")
    mx, mz = me // 4, me % 4
    f = lax.axis_index("fsdp")
    y, c = f // 2, f % 2
    sib = y * 2 + (1 - c)
    yup = ((y + 1) % 4) * 2 + c
    ydn = ((y + 3) % 4) * 2 + c
    far = ((y + 2) % 4) * 2 + c

    def peer(n):
        n = (n * 11) % PEERS
        return ((mx + n // 4) % 4) * 4 + (mz + n % 4) % 4

    def loop(n, body, lo=0):
        lax.fori_loop(lo, n, lambda i, _: (body(i), 0)[1], 0)

    def wrows(shard, off=0, n=SHARD):
        return pl.ds(pl.multiple_of(shard * SHARD + off, 128), n)

    def to_head(a, src, land, p):
        return pltpu.make_async_remote_copy(src.at[:, :, head_of(p)], land.at[rows_of(me)], send.at[a, p], recv.at[a, me],
                                            device_id={"seq": p}, device_id_type=MESH)

    def to_rows(a, src, land, p):
        return pltpu.make_async_remote_copy(src.at[rows_of(p)], land.at[:, :, head_of(me)], send.at[a, p], recv.at[a, me],
                                            device_id={"seq": p}, device_id_type=MESH)

    def got_head(a, src, land, p):
        pltpu.make_async_remote_copy(src.at[:, :, head_of(p)], land.at[rows_of(p)], send.at[a, p], recv.at[a, p],
                                     device_id={"seq": p}, device_id_type=MESH).wait_recv()

    def got_rows(a, src, land, p):
        pltpu.make_async_remote_copy(src.at[rows_of(p)], land.at[:, :, head_of(p)], send.at[a, p], recv.at[a, p],
                                     device_id={"seq": p}, device_id_type=MESH).wait_recv()

    def own_head(a, src, land):
        return pltpu.make_async_copy(src.at[:, :, head_of(me)], land.at[rows_of(me)], own.at[a])

    def own_rows(a, src, land):
        return pltpu.make_async_copy(src.at[rows_of(me)], land.at[:, :, head_of(me)], own.at[a])

    def wcopy(k, shard, target, src=None, off=0, n=SHARD):
        part = w_ref.at[wrows(shard, off, n)]
        return pltpu.make_async_remote_copy(part if src is None else src, part, wsend.at[k], wrecv.at[k],
                                            device_id={"fsdp": target}, device_id_type=MESH)

    dv_st, dk_st = k_ref, do_ref

    get_up = pltpu.make_async_copy(up_in, up_ref, lsem.at[0])
    get_up.start()
    get_w = pltpu.make_async_copy(w_in, w_ref.at[wrows(f)], lsem.at[1])
    get_w.start()

    barrier = pltpu.get_barrier_semaphore()
    loop(PEERS, lambda n: pl.semaphore_signal(barrier, inc=1, device_id={"seq": peer(n)}, device_id_type=MESH), 1)
    for t in (sib, yup, ydn):
        pl.semaphore_signal(barrier, inc=1, device_id={"fsdp": t}, device_id_type=MESH)
    pl.semaphore_wait(barrier, PEERS + 2)

    w_up = wcopy(0, f, yup, w_in)
    w_dn = wcopy(1, f, ydn, w_in)
    w_sib = wcopy(4, f, sib, w_in)
    w_up.start()
    w_dn.start()
    w_sib.start()
    for a, src, land in ((K_, k_in, k_ref), (V_, v_in, v_ref), (Q_, q_in, q_ref)):
        own_head(a, src, land).start()
        loop(PEERS, lambda n, a=a, src=src, land=land: to_head(a, src, land, peer(n)).start(), 1)

    fill_tables([text_tiles[u] for u in range(TXT)], near_ref, count_ref, pad_ref, keys_v, bias_v, pidx_v, tsel_v)
    moves = [pltpu.make_async_copy(a, b, lsem.at[2 + k]) for k, (a, b) in enumerate(
        ((keys_v, keys_ref), (bias_v, bias_ref), (pidx_v, pidx_ref), (tsel_v, tsel_ref)))]
    for move in moves:
        move.start()
    p_ref[TILES * SLOTS] = jnp.zeros((TILE, TILE), BF)
    get_up.wait()

    def scale_up(g):
        sl = pl.ds(pl.multiple_of(g * 32, 32), 32)
        sc_ref[sl, :] = (up_ref[sl, :].astype(F32) * gate_ref[...]).astype(BF)

    loop(ROWS // 32, scale_up)
    get_res = pltpu.make_async_copy(res_in, up_ref, lsem.at[0])
    get_res.start()

    def d_attn(shard):
        r = dot(sc_ref[...], w_ref[wrows(shard), :], NT).astype(BF)
        dst_ref[:, :, pl.ds(pl.multiple_of(shard * SHARD, SHARD), SHARD)] = r.reshape(OWN, TILE, SHARD)

    for move in moves:
        move.wait()
    get_w.wait()
    d_attn(f)
    w_sib.wait_recv()
    d_attn(sib)

    def turn(src, dst):
        def body(n):
            p = peer(n)
            for t in range(3):
                dst[p * 3 + t] = tile(src, p * 3 + t).T
        return body

    own_head(K_, k_in, k_ref).wait()
    loop(PEERS, lambda n: got_head(K_, k_in, k_ref, peer(n)), 1)
    loop(PEERS, turn(k_ref, kt_ref))
    w_up.wait_recv()
    fwd_up = wcopy(2, ydn, yup, None, 0, 128)
    fwd_up.start()
    sh_dn = wcopy(5, ydn, sib)
    sh_dn.start()
    w_dn.wait_recv()
    fwd_dn = wcopy(3, yup, ydn, None, 128, 128)
    fwd_dn.start()
    sh_up = wcopy(6, yup, sib)
    sh_up.start()
    d_attn(ydn)
    d_attn(yup)
    own_head(V_, v_in, v_ref).wait()
    loop(PEERS, lambda n: got_head(V_, v_in, v_ref, peer(n)), 1)
    loop(PEERS, turn(v_ref, vt_ref))
    sh_dn.wait_recv()
    d_attn(ydn + 1 - 2 * c)
    sh_up.wait_recv()
    d_attn(yup + 1 - 2 * c)
    own_head(Q_, q_in, q_ref).wait()
    loop(PEERS, lambda n: got_head(Q_, q_in, q_ref, peer(n)), 1)

    def stage(a, st, land, per_tile, lo=1, hi=PEERS + 1):
        def body(n):
            p = peer(n)
            for t in range(3):
                per_tile(p * 3 + t)

            @pl.when(n < PEERS)
            def _():
                to_rows(a, st, land, p).start()

        loop(hi, body, lo)
        if hi > PEERS:
            own_rows(a, st, land).start()

    def forward(lo, hi):
        def pair(k):
            a, b = peer(lo + 2 * k), peer(lo + 2 * k + 1)
            for p in (a, b):
                for t in range(3):
                    fwd_tile(p * 3 + t, q_ref, k_ref, vt_ref, keys_ref, bias_ref, p_ref, s_ref, inv_ref, at_st)
            to_rows(AT_, at_st, at_land, a).start()

            @pl.when(lo + 2 * k + 1 < PEERS)
            def _():
                to_rows(AT_, at_st, at_land, b).start()

        loop((hi - lo) // 2, pair)
        if hi > PEERS:
            own_rows(AT_, at_st, at_land).start()

    forward(1, 3)
    wcopy(2, far, yup, None, 0, 128).wait_recv()
    wcopy(3, far, yup, None, 128, 128).wait_recv()
    sh_far = wcopy(7, far, sib)
    sh_far.start()
    forward(3, 7)
    d_attn(far)
    sh_far.wait_recv()
    d_attn(far + 1 - 2 * c)
    loop(PEERS, lambda n: to_head(O_, dst_ref, do_ref, peer(n)).start(), 1)
    own_head(O_, dst_ref, do_ref).start()
    forward(7, PEERS + 1)
    own_head(O_, dst_ref, do_ref).wait()
    loop(PEERS, lambda n: got_head(O_, dst_ref, do_ref, peer(n)), 1)
    lax.fori_loop(0, TILES, lambda i, _: (scale_rows(i, do_ref, inv_ref, dq_st), 0)[1], 0, unroll=4)
    text_keys(p_ref, dq_st, text_ref)
    stage(DV_, dv_st, dv_out, lambda j: key_tile(j, keys_ref, pidx_ref, tsel_ref, p_ref, dq_st, text_ref, dv_st))
    stage(DQ_, dq_st, dq_out, lambda i: bwd_tile(i, v_ref, kt_ref, do_ref, at_st, keys_ref, p_ref, inv_ref, dq_st))
    text_keys(p_ref, q_ref, text_ref)
    stage(DK_, dk_st, dk_out, lambda j: key_tile(j, keys_ref, pidx_ref, tsel_ref, p_ref, q_ref, text_ref, dk_st))

    own_rows(AT_, at_st, at_land).wait()
    loop(PEERS, lambda n: got_rows(AT_, at_st, at_land, peer(n)), 1)
    get_res.wait()

    def project(g):
        sl = pl.ds(pl.multiple_of(g * 256, 256), 256)
        acc = dot(at_land[...].reshape(ROWS, HDT), w_ref[:, sl]) + obias_ref[:, sl]
        sc_ref[:, sl] = (up_ref[:, sl].astype(F32) + gate_ref[:, sl] * acc).astype(BF)

    loop(D // 256, project)

    outs = ((DV_, dv_st, dv_out), (DQ_, dq_st, dq_out), (DK_, dk_st, dk_out))
    for a, st, land in outs:
        own_rows(a, st, land).wait()
        loop(PEERS, lambda n, a=a, st=st, land=land: got_rows(a, st, land, peer(n)), 1)
    for cp in (w_up, w_dn, w_sib, fwd_up, fwd_dn, sh_dn, sh_up, sh_far):
        cp.wait_send()
    for a, src, land in ((K_, k_in, k_ref), (V_, v_in, v_ref), (Q_, q_in, q_ref), (O_, dst_ref, do_ref)):
        loop(PEERS, lambda n, a=a, src=src, land=land: to_head(a, src, land, peer(n)).wait_send(), 1)
    for a, st, land in ((AT_, at_st, at_land),) + outs:
        loop(PEERS, lambda n, a=a, st=st, land=land: to_rows(a, st, land, peer(n)).wait_send(), 1)


def local(queries, key_states, value_states, residual, upstream, mod_gate, out_bias, w_out, neighbours, counts, text_tiles):
    S, V, A = [pl.BlockSpec(memory_space=m) for m in (pltpu.SMEM, pltpu.VMEM, pl.ANY)]
    head = pltpu.VMEM((TILES, TILE, HD), BF)
    tok = pltpu.VMEM((ROWS, D), BF)
    mid = pltpu.VMEM((OWN, TILE, HDT), BF)
    dma = pltpu.SemaphoreType.DMA
    i32 = jnp.int32
    act = jax.ShapeDtypeStruct((OWN, TILE, HDT), BF)
    out, dq, dk, dv = pl.pallas_call(
        block_kernel,
        out_shape=[tok, mid, mid, mid],
        in_specs=[S] + [V] * 4 + [A] * 6,
        out_specs=[V] * 4,
        scratch_shapes=[head, head, head, head, mid, pltpu.VMEM((HDT, D), BF), tok, mid,
                        head, head,
                        pltpu.VMEM((TILES * SLOTS + 1, TILE, TILE), BF), pltpu.VMEM((SLOTS, TILE, TILE), F32),
                        pltpu.VMEM((TILES, TILE, TILE), BF), pltpu.VMEM((TILES, TILE, TILE), BF),
                        pltpu.VMEM((TILES, 1, TILE), F32), pltpu.VMEM((TXT + 1, TILE, TILE), F32),
                        *[m((n, TILE), t) for m in (pltpu.SMEM, pltpu.VMEM) for n, t in ((16, i32), (16, F32), (16, i32), (8, i32))],
                        pltpu.VMEM((TILE, TILE), i32),
                        dma((8, PEERS)), dma((8, PEERS)), dma((8,)), dma((8,)), dma((8,)), dma((6,))],
        compiler_params=pltpu.CompilerParams(collective_id=0, has_side_effects=True, vmem_limit_bytes=54 << 20),
        name="attention_block",
    )(text_tiles, neighbours.T, counts[None, :], mod_gate, out_bias[None, :],
      *[x.reshape(OWN, TILE, HDT) for x in (queries, key_states, value_states)], residual[0], upstream[0], w_out)
    return (out[None], *[x.reshape(1, ROWS, HDT) for x in (dq, dk, dv)])


def solution(mesh):
    act = P("fsdp", "seq", None)
    return jax.shard_map(local, mesh=mesh, in_specs=(act,) * 5 + (P("fsdp", None), P(), P("fsdp", None), P(), P(), P()),
                         out_specs=(act,) * 4, check_vma=False)
```

```python
import math
import jax, jax.numpy as jnp
from jax import lax
from jax.experimental import pallas as pl
from jax.experimental.pallas import tpu as pltpu
from jax.sharding import PartitionSpec as P

HD=128; TILE=128; TILES=48; NBR=9; TXT=4; SLOTS=13; D=3072; SEQ=6144; HDT=2048
FACTOR = 1.0/math.sqrt(HD)
EXP2 = FACTOR*math.log2(math.e)
F32=jnp.float32; BF=jnp.bfloat16

def fill_tables(text, near_ref, count_ref, pad_ref, keys_ref, bias_ref, pidx_ref, tsel_ref):
    pad_ref[...] = jnp.zeros((TILE, TILE), jnp.int32)
    near_t = near_ref[...]
    pad_ref[:NBR, :TILES] = near_t
    near = pad_ref[...].T[:TILES, :NBR]
    count_t = count_ref[...]
    pad_ref[:1, :TILES] = count_t
    count = pad_ref[...].T[:TILES, :1]
    query = lax.broadcasted_iota(jnp.int32, (TILES, TILES), 0)
    key = lax.broadcasted_iota(jnp.int32, (TILES, TILES), 1)
    block = jnp.zeros((TILES, TILES), jnp.int32)
    for s in range(NBR):
        block = jnp.where((near[:, s:s + 1] == key) & (s < count), query * SLOTS + s + 1, block)
    ids = lax.broadcasted_iota(jnp.int32, (1, TILES), 1)
    tsel = jnp.full((1, TILES), TXT, jnp.int32)
    for u in range(TXT):
        tsel = jnp.where(ids == text[u], u, tsel)
    tsel_ref[:1, :TILES] = tsel
    for r in range(SLOTS):
        live = r < count_t
        if r < NBR:
            who = near_t[r:r + 1, :]
            keys_ref[r:r + 1, :TILES] = jnp.where(live, who, near_t[:1, :])
            bias_ref[r:r + 1, :TILES] = jnp.where(live, 0.0, -jnp.inf).astype(F32)
        else:
            who = jnp.full((1, TILES), text[r - NBR], jnp.int32)
            keys_ref[r:r + 1, :TILES] = who
        pick = jnp.sum(jnp.where(query == who, block, 0), axis=0, keepdims=True)
        ok = (pick > 0) & (tsel == TXT)
        if r < NBR:
            ok = ok & live
        pidx_ref[r:r + 1, :TILES] = jnp.where(ok, pick - 1, TILES * SLOTS)


def tile(ref, i):
    return ref[i]

NT = (((1,), (1,)), ((), ()))
NN = (((1,), (0,)), ((), ()))

def dot(a, b, dims=NN):
    return lax.dot_general(a, b, dims, preferred_element_type=F32)

def fwd_tile(i, q_ref, k_ref, vt_ref, keys_ref, bias_ref, p_ref, s_ref, inv_ref, attn_ref):
    q = tile(q_ref, i)
    top = None
    kc = jnp.concatenate([tile(k_ref, keys_ref[s, i]) for s in range(SLOTS)], axis=0)
    sall = dot(kc, q, NT).reshape(SLOTS, TILE, TILE)
    for s in range(SLOTS):
        sc = sall[s]
        s_ref[s] = sc
        top = sc if top is None else jnp.maximum(top, sc)
    m = jnp.max(top, axis=0, keepdims=True) * EXP2
    total = None
    parts = []
    for s in range(SLOTS):
        shift = m if s < 3 or s >= NBR else m - bias_ref[s, i]
        e = jnp.exp2(s_ref[s] * EXP2 - shift)
        total = e if total is None else total + e
        e16 = e.astype(BF)
        p_ref[i * SLOTS + s] = e16
        parts.append(e16)
    inv = 1.0 / jnp.sum(total, axis=0, keepdims=True)
    inv_ref[i] = inv
    pt = jnp.concatenate(parts, axis=0)
    vt = jnp.concatenate([vt_ref[keys_ref[s, i]] for s in range(SLOTS)], axis=1)
    attn_t = dot(vt, pt) * inv
    attn_ref[i] = attn_t.astype(BF).T

def key_tile(j, who_ref, pidx_ref, tsel_ref, p_ref, x_ref, text_ref, out_ref):
    lhs = jnp.concatenate([p_ref[pidx_ref[r, j]] for r in range(SLOTS)], axis=1)
    rhs = jnp.concatenate([tile(x_ref, who_ref[r, j]) for r in range(SLOTS)], axis=0)
    acc = dot(lhs, rhs) + text_ref[tsel_ref[0, j]]
    out_ref[j] = acc.astype(BF)

def text_keys(p_ref, x_ref, text_ref):
    G = 12
    text_ref[...] = jnp.zeros_like(text_ref)
    def body(g, _):
        rhs = x_ref[pl.ds(g * G, G)].reshape(G * TILE, HD)
        for u in range(TXT):
            lhs = jnp.concatenate([p_ref[(g * G + n) * SLOTS + NBR + u] for n in range(G)], axis=1)
            text_ref[u] += dot(lhs, rhs)
        return 0
    lax.fori_loop(0, TILES // G, body, 0)

def bwd_tile(i, v_ref, kt_ref, do_ref, attn_ref, keys_ref, p_ref, inv_ref, dq_ref):
    do = tile(do_ref, i)
    prod = do.astype(F32) * tile(attn_ref, i).astype(F32)
    delta = jnp.sum(prod.T, axis=0, keepdims=True)
    c = inv_ref[i] * FACTOR
    dc = delta * c
    vc = jnp.concatenate([tile(v_ref, keys_ref[s, i]) for s in range(SLOTS)], axis=0)
    dpall = dot(vc, do, NT).reshape(SLOTS, TILE, TILE)
    parts = [(p_ref[i * SLOTS + s].astype(F32) * (dpall[s] * c - dc)).astype(BF) for s in range(SLOTS)]
    for s in range(SLOTS): p_ref[i * SLOTS + s] = parts[s]
    ds = jnp.concatenate(parts, axis=0)
    kt = jnp.concatenate([kt_ref[keys_ref[s, i]] for s in range(SLOTS)], axis=1)
    dq_t = dot(kt, ds)
    dq_ref[i] = dq_t.astype(BF).T

def scale_rows(i, do_ref, inv_ref, dos_ref):
    col = jnp.broadcast_to(inv_ref[i], (TILE, TILE)).T
    dos_ref[i] = (do_ref[i].astype(F32) * col).astype(BF)


MESH = pl.DeviceIdType.MESH
PEERS = 16
ROWS = SEQ // PEERS
SHARD = 256
OWN = TILES // PEERS
K_, V_, Q_, O_, AT_, DV_, DQ_, DK_ = range(8)


def rows_of(p):
    return pl.ds(p * OWN, OWN)


def head_of(p):
    return pl.ds(pl.multiple_of(p * HD, HD), HD)


def block_kernel(text_tiles, near_ref, count_ref, gate_ref, obias_ref,
                 q_in, k_in, v_in, res_in, up_in, w_in,
                 sc_ref, dq_out, dk_out, dv_out,
                 q_ref, k_ref, v_ref, do_ref, at_land, w_ref, up_ref, dst_ref,
                 at_st, dq_st,
                 p_ref, s_ref, kt_ref, vt_ref, inv_ref, text_ref,
                 keys_ref, bias_ref, pidx_ref, tsel_ref, keys_v, bias_v, pidx_v, tsel_v, pad_ref,
                 send, recv, own, wsend, wrecv, lsem):
    me = lax.axis_index("seq")
    mx, mz = me // 4, me % 4
    f = lax.axis_index("fsdp")
    y, c = f // 2, f % 2
    sib = y * 2 + (1 - c)
    yup = ((y + 1) % 4) * 2 + c
    ydn = ((y + 3) % 4) * 2 + c
    far = ((y + 2) % 4) * 2 + c

    def peer(n):
        n = (n * 11) % PEERS
        return ((mx + n // 4) % 4) * 4 + (mz + n % 4) % 4

    def loop(n, body, lo=0):
        lax.fori_loop(lo, n, lambda i, _: (body(i), 0)[1], 0)

    def wrows(shard, off=0, n=SHARD):
        return pl.ds(pl.multiple_of(shard * SHARD + off, 128), n)

    def to_head(a, src, land, p):
        return pltpu.make_async_remote_copy(src.at[:, :, head_of(p)], land.at[rows_of(me)], send.at[a, p], recv.at[a, me],
                                            device_id={"seq": p}, device_id_type=MESH)

    def to_rows(a, src, land, p):
        return pltpu.make_async_remote_copy(src.at[rows_of(p)], land.at[:, :, head_of(me)], send.at[a, p], recv.at[a, me],
                                            device_id={"seq": p}, device_id_type=MESH)

    def got_head(a, src, land, p):
        pltpu.make_async_remote_copy(src.at[:, :, head_of(p)], land.at[rows_of(p)], send.at[a, p], recv.at[a, p],
                                     device_id={"seq": p}, device_id_type=MESH).wait_recv()

    def got_rows(a, src, land, p):
        pltpu.make_async_remote_copy(src.at[rows_of(p)], land.at[:, :, head_of(p)], send.at[a, p], recv.at[a, p],
                                     device_id={"seq": p}, device_id_type=MESH).wait_recv()

    def own_head(a, src, land):
        return pltpu.make_async_copy(src.at[:, :, head_of(me)], land.at[rows_of(me)], own.at[a])

    def own_rows(a, src, land):
        return pltpu.make_async_copy(src.at[rows_of(me)], land.at[:, :, head_of(me)], own.at[a])

    def wcopy(k, shard, target, src=None, off=0, n=SHARD):
        part = w_ref.at[wrows(shard, off, n)]
        return pltpu.make_async_remote_copy(part if src is None else src, part, wsend.at[k], wrecv.at[k],
                                            device_id={"fsdp": target}, device_id_type=MESH)

    dv_st, dk_st = k_ref, do_ref

    get_up = pltpu.make_async_copy(up_in, up_ref, lsem.at[0])
    get_up.start()
    get_w = pltpu.make_async_copy(w_in, w_ref.at[wrows(f)], lsem.at[1])
    get_w.start()

    barrier = pltpu.get_barrier_semaphore()
    loop(PEERS, lambda n: pl.semaphore_signal(barrier, inc=1, device_id={"seq": peer(n)}, device_id_type=MESH), 1)
    for t in (sib, yup, ydn):
        pl.semaphore_signal(barrier, inc=1, device_id={"fsdp": t}, device_id_type=MESH)
    pl.semaphore_wait(barrier, PEERS + 2)

    w_up = wcopy(0, f, yup, w_in)
    w_dn = wcopy(1, f, ydn, w_in)
    w_sib = wcopy(4, f, sib, w_in)
    w_up.start()
    w_dn.start()
    w_sib.start()
    for a, src, land in ((K_, k_in, k_ref), (V_, v_in, v_ref), (Q_, q_in, q_ref)):
        own_head(a, src, land).start()
        loop(PEERS, lambda n, a=a, src=src, land=land: to_head(a, src, land, peer(n)).start(), 1)

    fill_tables([text_tiles[u] for u in range(TXT)], near_ref, count_ref, pad_ref, keys_v, bias_v, pidx_v, tsel_v)
    moves = [pltpu.make_async_copy(a, b, lsem.at[2 + k]) for k, (a, b) in enumerate(
        ((keys_v, keys_ref), (bias_v, bias_ref), (pidx_v, pidx_ref), (tsel_v, tsel_ref)))]
    for move in moves:
        move.start()
    p_ref[TILES * SLOTS] = jnp.zeros((TILE, TILE), BF)
    get_up.wait()

    def scale_up(g):
        sl = pl.ds(pl.multiple_of(g * 32, 32), 32)
        sc_ref[sl, :] = (up_ref[sl, :].astype(F32) * gate_ref[...]).astype(BF)

    loop(ROWS // 32, scale_up)
    get_res = pltpu.make_async_copy(res_in, up_ref, lsem.at[0])
    get_res.start()

    def d_attn(shard):
        r = dot(sc_ref[...], w_ref[wrows(shard), :], NT).astype(BF)
        dst_ref[:, :, pl.ds(pl.multiple_of(shard * SHARD, SHARD), SHARD)] = r.reshape(OWN, TILE, SHARD)

    for move in moves:
        move.wait()
    get_w.wait()
    d_attn(f)
    w_sib.wait_recv()
    d_attn(sib)

    def turn(src, dst):
        def body(n):
            p = peer(n)
            for t in range(3):
                dst[p * 3 + t] = tile(src, p * 3 + t).T
        return body

    own_head(K_, k_in, k_ref).wait()
    loop(PEERS, lambda n: got_head(K_, k_in, k_ref, peer(n)), 1)
    loop(PEERS, turn(k_ref, kt_ref))
    w_up.wait_recv()
    fwd_up = wcopy(2, ydn, yup, None, 0, 128)
    fwd_up.start()
    sh_dn = wcopy(5, ydn, sib)
    sh_dn.start()
    w_dn.wait_recv()
    fwd_dn = wcopy(3, yup, ydn, None, 128, 128)
    fwd_dn.start()
    sh_up = wcopy(6, yup, sib)
    sh_up.start()
    d_attn(ydn)
    d_attn(yup)
    own_head(V_, v_in, v_ref).wait()
    loop(PEERS, lambda n: got_head(V_, v_in, v_ref, peer(n)), 1)
    loop(PEERS, turn(v_ref, vt_ref))
    sh_dn.wait_recv()
    d_attn(ydn + 1 - 2 * c)
    sh_up.wait_recv()
    d_attn(yup + 1 - 2 * c)
    own_head(Q_, q_in, q_ref).wait()
    loop(PEERS, lambda n: got_head(Q_, q_in, q_ref, peer(n)), 1)

    def stage(a, st, land, per_tile, lo=1, hi=PEERS + 1):
        def pair(k):
            a_p, b_p = peer(lo + 2 * k), peer(lo + 2 * k + 1)
            for p in (a_p, b_p):
                for t in range(3):
                    per_tile(p * 3 + t)
            to_rows(a, st, land, a_p).start()

            @pl.when(lo + 2 * k + 1 < PEERS)
            def _():
                to_rows(a, st, land, b_p).start()

        loop((hi - lo) // 2, pair)
        if hi > PEERS:
            own_rows(a, st, land).start()

    def forward(lo, hi):
        stage(AT_, at_st, at_land, lambda i: fwd_tile(i, q_ref, k_ref, vt_ref, keys_ref, bias_ref, p_ref, s_ref, inv_ref, at_st), lo, hi)

    forward(1, 3)
    wcopy(2, far, yup, None, 0, 128).wait_recv()
    wcopy(3, far, yup, None, 128, 128).wait_recv()
    sh_far = wcopy(7, far, sib)
    sh_far.start()
    forward(3, 7)
    d_attn(far)
    sh_far.wait_recv()
    d_attn(far + 1 - 2 * c)
    loop(PEERS, lambda n: to_head(O_, dst_ref, do_ref, peer(n)).start(), 1)
    own_head(O_, dst_ref, do_ref).start()
    forward(7, PEERS + 1)
    own_head(O_, dst_ref, do_ref).wait()
    loop(PEERS, lambda n: got_head(O_, dst_ref, do_ref, peer(n)), 1)
    lax.fori_loop(0, TILES, lambda i, _: (scale_rows(i, do_ref, inv_ref, dq_st), 0)[1], 0, unroll=4)
    text_keys(p_ref, dq_st, text_ref)
    stage(DV_, dv_st, dv_out, lambda j: key_tile(j, keys_ref, pidx_ref, tsel_ref, p_ref, dq_st, text_ref, dv_st))
    stage(DQ_, dq_st, dq_out, lambda i: bwd_tile(i, v_ref, kt_ref, do_ref, at_st, keys_ref, p_ref, inv_ref, dq_st))
    text_keys(p_ref, q_ref, text_ref)
    stage(DK_, dk_st, dk_out, lambda j: key_tile(j, keys_ref, pidx_ref, tsel_ref, p_ref, q_ref, text_ref, dk_st))

    own_rows(AT_, at_st, at_land).wait()
    loop(PEERS, lambda n: got_rows(AT_, at_st, at_land, peer(n)), 1)
    get_res.wait()

    def project(g):
        sl = pl.ds(pl.multiple_of(g * 256, 256), 256)
        acc = dot(at_land[...].reshape(ROWS, HDT), w_ref[:, sl]) + obias_ref[:, sl]
        sc_ref[:, sl] = (up_ref[:, sl].astype(F32) + gate_ref[:, sl] * acc).astype(BF)

    loop(D // 256, project)

    outs = ((DV_, dv_st, dv_out), (DQ_, dq_st, dq_out), (DK_, dk_st, dk_out))
    for a, st, land in outs:
        own_rows(a, st, land).wait()
        loop(PEERS, lambda n, a=a, st=st, land=land: got_rows(a, st, land, peer(n)), 1)
    for cp in (w_up, w_dn, w_sib, fwd_up, fwd_dn, sh_dn, sh_up, sh_far):
        cp.wait_send()
    for a, src, land in ((K_, k_in, k_ref), (V_, v_in, v_ref), (Q_, q_in, q_ref), (O_, dst_ref, do_ref)):
        loop(PEERS, lambda n, a=a, src=src, land=land: to_head(a, src, land, peer(n)).wait_send(), 1)
    for a, st, land in ((AT_, at_st, at_land),) + outs:
        loop(PEERS, lambda n, a=a, st=st, land=land: to_rows(a, st, land, peer(n)).wait_send(), 1)


def local(queries, key_states, value_states, residual, upstream, mod_gate, out_bias, w_out, neighbours, counts, text_tiles):
    S, V, A = [pl.BlockSpec(memory_space=m) for m in (pltpu.SMEM, pltpu.VMEM, pl.ANY)]
    head = pltpu.VMEM((TILES, TILE, HD), BF)
    tok = pltpu.VMEM((ROWS, D), BF)
    mid = pltpu.VMEM((OWN, TILE, HDT), BF)
    dma = pltpu.SemaphoreType.DMA
    i32 = jnp.int32
    act = jax.ShapeDtypeStruct((OWN, TILE, HDT), BF)
    out, dq, dk, dv = pl.pallas_call(
        block_kernel,
        out_shape=[tok, mid, mid, mid],
        in_specs=[S] + [V] * 4 + [A] * 6,
        out_specs=[V] * 4,
        scratch_shapes=[head, head, head, head, mid, pltpu.VMEM((HDT, D), BF), tok, mid,
                        head, head,
                        pltpu.VMEM((TILES * SLOTS + 1, TILE, TILE), BF), pltpu.VMEM((SLOTS, TILE, TILE), F32),
                        pltpu.VMEM((TILES, TILE, TILE), BF), pltpu.VMEM((TILES, TILE, TILE), BF),
                        pltpu.VMEM((TILES, 1, TILE), F32), pltpu.VMEM((TXT + 1, TILE, TILE), F32),
                        *[m((n, TILE), t) for m in (pltpu.SMEM, pltpu.VMEM) for n, t in ((16, i32), (16, F32), (16, i32), (8, i32))],
                        pltpu.VMEM((TILE, TILE), i32),
                        dma((8, PEERS)), dma((8, PEERS)), dma((8,)), dma((8,)), dma((8,)), dma((6,))],
        compiler_params=pltpu.CompilerParams(collective_id=0, has_side_effects=True, vmem_limit_bytes=54 << 20),
        name="attention_block",
    )(text_tiles, neighbours.T, counts[None, :], mod_gate, out_bias[None, :],
      *[x.reshape(OWN, TILE, HDT) for x in (queries, key_states, value_states)], residual[0], upstream[0], w_out)
    return (out[None], *[x.reshape(1, ROWS, HDT) for x in (dq, dk, dv)])


def solution(mesh):
    act = P("fsdp", "seq", None)
    return jax.shard_map(local, mesh=mesh, in_specs=(act,) * 5 + (P("fsdp", None), P(), P("fsdp", None), P(), P(), P()),
                         out_specs=(act,) * 4, check_vma=False)
```
